128 devices in a mesh: pu: 8 (over y, core), pv: 16 (over z, x).
Axes of the slice: x: 4, y: 4, z: 4, core: 2. Of those that a mesh axis runs over, the one named last changes fastest.
Arguments:
- density: bfloat16 [48, 96, 128, 768], P('pu', 'pv'), may hold values from -6 to 6
- near_blocks: bfloat16 [48, 96, 6, 128, 128], P('pu', 'pv'), may hold values from -0.21875 to 0.21875
- neighbours: int32 [48, 96, 6], P('pu', 'pv'), may hold values from 0 to 9
- far_right: bfloat16 [48, 96, 128, 128], P('pu', 'pv'), may hold values from -0.09375 to 0.09375
- far_left: float32 [8, 16, 1024, 128], P('pu', 'pv'), may hold values from -0.1875 to 0.1875
- sketch: float32 [256, 128], replicated, may hold values from -0.375 to 0.375
- patch_order: int32 [128], replicated, may hold values from 0 to 127, each once
Outputs:
- corrected: bfloat16 [48, 96, 128, 768], P('pu', 'pv')
- far_field: float32 [1024, 768], P('pu', 'pv')
The draws below stay inside these ranges and needn't reach their ends.
Inputs may be any that keep to these rules, and one draw needn't show every extreme that they name: `neighbours`: entry e < 9 names the block displaced by e // 3 - 1 patch rows and e % 3 - 1 patch columns (e = 4 is the block itself); 9 marks an empty slot. `patch_order`: A permutation of the patches.
All inputs are finite; a program needn't handle non-finite values.
Results may differ from the reference program's by a relative error of at most 0.0028.
Values may be sent and summed in bfloat16 or wider, within the bound.
A program may use at most 256 MiB of HBM per device.

```python
import jax
import jax.numpy as jnp
from jax import lax

BLK = 64
SLOTS = 6
GU = 6
GV = 6
RHS = 768
OBS = 1024
RANK = 128
NBU = 48
NBV = 96
N_PU = 8
N_PV = 16
DEVICES = 128


def plant(drawn, rng, least, high):
    longest = drawn.shape.index(max(drawn.shape))
    spots = []
    for shift in (0, 1):
        where = [jax.random.randint(jax.random.fold_in(rng, axis), (), 0, length) for axis, length in enumerate(drawn.shape)]
        where[longest] = (where[longest] + shift) % drawn.shape[longest]
        spots.append(tuple(where))
    return drawn.at[spots[0]].set(least).at[spots[1]].set(high)


def levels(own_key, dims, split, least, top_value):
    factor_of = 1.0
    for axis_at, parts in split:
        draws = jax.random.uniform(jax.random.fold_in(jax.random.fold_in(own_key, 6), axis_at), (parts,), jnp.float32, least / len(split), top_value / len(split))
        factor_of = factor_of * jnp.repeat(jnp.exp(draws), dims[axis_at] // parts).reshape((-1,) + (1,) * (len(dims) - 1 - axis_at))
    return factor_of


def scatter_about(key, extent, spread, bound, pieces=(), held_as=jnp.bfloat16):
    drawn = spread * jax.random.normal(key, extent, jnp.float32)
    if pieces:
        drawn = drawn * levels(key, extent, pieces, -0.22, 0.18)
    return jnp.clip(drawn, -bound, bound).astype(held_as)


def setup_inputs(seed: int = 0) -> dict:
    seeds = jax.random.split(jax.random.key(seed), 8)
    density = scatter_about(seeds[0], (NBU, NBV, 2 * BLK, RHS), 1.0, 6.0, ((0, 8), (1, 16)))
    near_blocks = scatter_about(seeds[1], (NBU, NBV, SLOTS, 2 * BLK, 2 * BLK), (2 * BLK * SLOTS) ** -0.5, 0.21875, ((0, 8), (1, 16)))
    neighbours = plant(jax.random.randint(seeds[2], (NBU, NBV, SLOTS), 0, 10), jax.random.fold_in(seeds[2], 1), 0, 9).astype(jnp.int32)
    far_right = scatter_about(seeds[3], (NBU, NBV, 2 * BLK, RANK), (GU * GV * 2 * BLK) ** -0.5, 0.09375, ((0, 8), (1, 16)))
    far_left = scatter_about(seeds[4], (N_PU, N_PV, OBS, RANK), OBS ** -0.5, 0.1875, ((0, 8), (1, 16)), jnp.float32)
    sketch = scatter_about(seeds[5], (2 * RANK, RANK), (2 * RANK) ** -0.5, 0.375, (), jnp.float32)
    patch_order = jax.random.permutation(seeds[6], DEVICES).astype(jnp.int32)
    return dict(density=density, near_blocks=near_blocks, neighbours=neighbours, far_right=far_right, far_left=far_left, sketch=sketch, patch_order=patch_order)


highest = lax.Precision.HIGHEST
empty_slot = 9

def merge_pair(first_left, first_coef, second_left, second_coef, sketch):
    stacked = jnp.concatenate([first_left, second_left], axis=1)
    coeff_pairs = jnp.concatenate([first_coef, second_coef], axis=0)
    gram_matrix = jnp.dot(stacked.T, stacked, precision=highest)
    reduced = jnp.dot(sketch.T, gram_matrix, precision=highest)
    inner_gram = jnp.dot(reduced, sketch, precision=highest)
    inner_gram = 0.5 * (inner_gram + inner_gram.T)
    factor = jnp.linalg.cholesky(inner_gram)
    sketched = jnp.dot(stacked, sketch, precision=highest)
    new_left = lax.linalg.triangular_solve(factor, sketched.T, left_side=True, lower=True).T
    new_coef = lax.linalg.triangular_solve(factor, jnp.dot(reduced, coeff_pairs, precision=highest), left_side=True, lower=True)
    return (new_left, new_coef)

def local_tree(left_stack, coef_stack, group_keys, sketch):
    while left_stack.shape[0] > 1:
        half_count = left_stack.shape[0] // 2
        left_pairs = left_stack.reshape((half_count, 2) + left_stack.shape[1:])
        coef_pairs = coef_stack.reshape((half_count, 2) + coef_stack.shape[1:])
        key_pairs = group_keys.reshape(half_count, 2)
        first_mask = (key_pairs[:, 0] < key_pairs[:, 1])[:, None, None]
        first_left = jnp.where(first_mask, left_pairs[:, 0], left_pairs[:, 1])
        second_left = jnp.where(first_mask, left_pairs[:, 1], left_pairs[:, 0])
        first_coef = jnp.where(first_mask, coef_pairs[:, 0], coef_pairs[:, 1])
        second_coef = jnp.where(first_mask, coef_pairs[:, 1], coef_pairs[:, 0])
        left_stack, coef_stack = jax.vmap(merge_pair, in_axes=(0, 0, 0, 0, None))(first_left, first_coef, second_left, second_coef, sketch)
        group_keys = key_pairs.min(axis=1)
    return (left_stack[0], coef_stack[0])

def reference(density, near_blocks, neighbours, far_right, far_left, sketch, patch_order):
    padded = jnp.pad(density, ((1, 1), (1, 1), (0, 0), (0, 0)))
    col_base = jnp.arange(NBV).astype(jnp.int32)

    def one_row(row_index):
        slab = lax.dynamic_slice_in_dim(padded, row_index, 3, 0)
        blocks_row = lax.dynamic_index_in_dim(near_blocks, row_index, 0, keepdims=False)
        links_row = lax.dynamic_index_in_dim(neighbours, row_index, 0, keepdims=False)
        density_row = lax.dynamic_index_in_dim(density, row_index, 0, keepdims=False)
        summed = jnp.zeros(density_row.shape, jnp.float32)
        for position in range(SLOTS):
            slot_links = links_row[:, position]
            stencil = jnp.minimum(slot_links, 8)
            near_rows = slab[stencil // 3, col_base + stencil % 3]
            product = jnp.einsum('jab,jbr->jar', blocks_row[:, position].astype(jnp.float32), near_rows.astype(jnp.float32))
            summed = summed + jnp.where((slot_links < empty_slot)[:, None, None], product, 0.0)
        return (density_row.astype(jnp.float32) + summed).astype(jnp.bfloat16)
    corrected = lax.map(one_row, jnp.arange(NBU).astype(jnp.int32))

    def patch_coeffs(patch_row):
        rows_here = lax.dynamic_slice_in_dim(corrected, patch_row * GU, GU, 0).reshape(GU, N_PV, GV, 2 * BLK, RHS)
        right_here = lax.dynamic_slice_in_dim(far_right, patch_row * GU, GU, 0).reshape(GU, N_PV, GV, 2 * BLK, RANK)
        return jnp.einsum('ivjar,ivjak->vrk', right_here.astype(jnp.float32), rows_here.astype(jnp.float32))
    coeffs = lax.map(patch_coeffs, jnp.arange(N_PU).astype(jnp.int32))
    key_grid = patch_order.reshape(N_PU, N_PV)
    row_left, row_coef = jax.vmap(local_tree, in_axes=(0, 0, 0, None))(far_left, coeffs, key_grid, sketch)
    root_left, root_coef = local_tree(row_left, row_coef, key_grid.min(axis=1), sketch)
    far_field = jnp.dot(root_left, root_coef, precision=highest)
    return (corrected, far_field)
```

```python
import functools

import jax
import jax.numpy as jnp
from jax import lax
from jax.experimental import pallas as pl
from jax.experimental.pallas import tpu as pltpu
from jax.sharding import PartitionSpec as P

MESH = pl.DeviceIdType.MESH
highest = lax.Precision.HIGHEST
f32 = jnp.float32
LEVELS = 7


def dot_nn(a, b):
    return lax.dot_general(a, b, (((1,), (0,)), ((), ())), precision=highest, preferred_element_type=f32)


def dot_tn(a, b):
    return lax.dot_general(a, b, (((0,), (0,)), ((), ())), precision=highest, preferred_element_type=f32)


def dot_nt(a, b):
    return lax.dot_general(a, b, (((1,), (1,)), ((), ())), precision=highest, preferred_element_type=f32)


def tile(x):
    return jnp.broadcast_to(x, (8, 128))


def cholesky_inverse(gram, out_ref):
    groups = 16
    row = lax.broadcasted_iota(jnp.int32, (8, 128), 0)
    lane = lax.broadcasted_iota(jnp.int32, (8, 128), 1)
    left = [gram[8 * g : 8 * g + 8, :] for g in range(groups)]
    right = [jnp.where(lane == row + 8 * g, 1.0, 0.0).astype(f32) for g in range(groups)]
    for b in range(groups):
        base = 8 * b
        last = b == groups - 1
        cols = [[tile(left[g][:, base + k : base + k + 1]) for k in range(8)] for g in range(b, groups)]
        d = [[tile(cols[0][k][i : i + 1, :]) for k in range(i + 1)] for i in range(8)]
        low = [[None] * 8 for _ in range(8)]
        inv = [[None] * 8 for _ in range(8)]
        for k in range(8):
            scale = lax.rsqrt(d[k][k])
            for i in range(k + 1, 8):
                low[i][k] = d[i][k] * scale
            for m in range(k + 1, 8):
                for i in range(m, 8):
                    d[i][m] = d[i][m] - low[i][k] * low[m][k]
            inv[k][k] = scale
            for j in range(k):
                s = low[k][j] * inv[j][j]
                for q in range(j + 1, k):
                    s = s + low[k][q] * inv[q][j]
                inv[k][j] = -(scale * s)

        def solved(panel):
            up = []
            for i in range(8):
                s = inv[i][0] * panel[0]
                for k in range(1, i + 1):
                    s = s + inv[i][k] * panel[k]
                up.append(s)
            return up

        def solved_again(up):
            full = []
            for k in range(8):
                s = inv[k][k] * up[k]
                for i in range(k + 1, 8):
                    s = s + inv[i][k] * up[i]
                full.append(s)
            return full

        up_right = solved([tile(right[b][k : k + 1, :]) for k in range(8)])
        for i in range(8):
            out_ref[base + i : base + i + 1, :] = up_right[i][0:1, :]
        if last:
            break
        full_left = solved_again(solved([tile(left[b][k : k + 1, :]) for k in range(8)]))
        full_right = solved_again(up_right)
        for g in range(b + 1, groups):
            c = cols[g - b]
            drop_left = c[0] * full_left[0]
            drop_right = c[0] * full_right[0]
            for k in range(1, 8):
                drop_left = drop_left + c[k] * full_left[k]
                drop_right = drop_right + c[k] * full_right[k]
            left[g] = left[g] - drop_left
            right[g] = right[g] - drop_right


def flip(index, bit):
    return index + bit - 2 * bit * ((index // bit) % 2)


def tree_kernel(
    leaf, sketch, keys, path_out, root_out,
    mine, other, w_mine, w_other, halves, gram_send, gram_recv, gram, linv, path, before, swap,
    leaf_local, leaf_send, leaf_recv, y_send, y_recv, w_send, w_recv, g_send, g_recv, s_send, s_recv,
):
    u = lax.axis_index("pu")
    v = lax.axis_index("pv")
    core = u % 2
    y = u // 2
    x0 = v % 2
    u_core = flip(u, 1)
    v_next = flip(v, 1)
    partners = {1: (u, flip(v, 2)), 2: (u, flip(v, 4)), 3: (u, flip(v, 8)), 4: (u, v_next), 5: (flip(u, 2), v), 6: (flip(u, 4), v)}
    barrier = pltpu.get_barrier_semaphore()
    peers = list(partners.values()) + [(u_core, v), (u_core, v_next)]
    for peer in peers:
        pl.semaphore_signal(barrier, inc=1, device_id=peer, device_id_type=MESH)
    pl.semaphore_wait(barrier, len(peers))

    def leaf_copy(part, slot_ref, to, slot):
        return pltpu.make_async_remote_copy(
            src_ref=leaf.at[:, part], dst_ref=slot_ref.at[0], send_sem=leaf_send.at[part],
            recv_sem=leaf_recv.at[slot], device_id=to, device_id_type=MESH,
        )

    slots = (mine, other)
    for c in range(2):
        for x in range(2):
            @pl.when((core == c) & (x0 == x))
            def _(c=c, x=x):
                if c == x:
                    local = pltpu.make_async_copy(leaf.at[:, c], slots[x].at[0], leaf_local)
                    local.start()
                    leaf_copy(1 - c, slots[x], (u_core, v), x).start()
                    local.wait()
                else:
                    leaf_copy(c, slots[x], (u, v_next), x).start()
                    leaf_copy(1 - c, slots[x], (u_core, v_next), x).start()

    key = keys[...]
    rows = lax.broadcasted_iota(jnp.int32, (8, 16), 0)
    cols = lax.broadcasted_iota(jnp.int32, (8, 16), 1)
    host_row = 2 * y + x0

    def least(mask):
        return jnp.min(jnp.min(jnp.where(mask, key, 1 << 20), axis=1, keepdims=True), axis=0, keepdims=True)

    here = rows == host_row
    even = v - x0
    pairs = [(here & (cols == even), here & (cols == even + 1))]
    for bit in (2, 4, 8):
        pairs.append((here & (cols // bit == v // bit), here & (cols // bit == flip(v, bit) // bit)))
    pairs.append((here, rows == 2 * y + 1 - x0))
    for bit in (2, 4):
        pairs.append((rows // bit == u // bit, rows // bit == flip(u, bit) // bit))
    first = sketch[0:128, :]
    second = sketch[128:256, :]
    for t, (own, sibling) in enumerate(pairs):
        leads = jnp.broadcast_to((least(own) < least(sibling)).astype(f32), (128, 128)) > 0.5
        halves[t] = jnp.where(leads, first, second)
        if t == 0:
            w_mine[0] = halves[0]
            w_other[0] = jnp.where(leads, second, first)
    diag = lax.broadcasted_iota(jnp.int32, (128, 128), 0) == lax.broadcasted_iota(jnp.int32, (128, 128), 1)
    before[...] = jnp.where(diag, 1.0, 0.0).astype(f32)

    for c in range(2):
        for x in range(2):
            @pl.when((core == c) & (x0 == x))
            def _(c=c, x=x):
                if c == x:
                    leaf_copy(1 - c, slots[x], (u_core, v), x).wait_send()
                    leaf_copy(0, slots[1 - x], (u_core, v), 1 - x).wait_recv()
                else:
                    for part in range(2):
                        leaf_copy(part, slots[x], (u_core, v), x).wait_send()
                    for slot in range(2):
                        leaf_copy(0, slots[slot], (u_core, v), slot).wait_recv()

    def y_copy(t, to):
        return pltpu.make_async_remote_copy(
            src_ref=mine.at[t + 1], dst_ref=other.at[t + 1], send_sem=y_send.at[t], recv_sem=y_recv.at[t],
            device_id=to, device_id_type=MESH,
        )

    def w_copy(t, to):
        return pltpu.make_async_remote_copy(
            src_ref=w_mine.at[t + 1], dst_ref=w_other.at[t + 1], send_sem=w_send.at[t], recv_sem=w_recv.at[t],
            device_id=to, device_id_type=MESH,
        )

    def g_copy(t, kind):
        return pltpu.make_async_remote_copy(
            src_ref=gram_send.at[t, kind], dst_ref=gram_recv.at[t, kind], send_sem=g_send.at[t, kind],
            recv_sem=g_recv.at[t, kind], device_id=(u_core, v), device_id_type=MESH,
        )

    def swap_copy():
        return pltpu.make_async_remote_copy(
            src_ref=path, dst_ref=swap, send_sem=s_send, recv_sem=s_recv,
            device_id=(u_core, v_next), device_id_type=MESH,
        )

    def merge(t, carry):
        for r in range(4):
            part = (t, r)
            mine[t + 1, r] = dot_nn(mine[part], w_mine[t]) + dot_nn(other[part], w_other[t])
        for step in range(LEVELS - 1):
            @pl.when(t == step)
            def _(step=step):
                y_copy(step, partners[step + 1]).start()
        merged = mine[t + 1].reshape(512, 128)
        part_gram = dot_tn(merged, merged)
        gram_send[t, 0] = part_gram
        g_copy(t, 0).start()
        part_cross = dot_tn(merged, mine[t].reshape(512, 128))
        gram_send[t, 1] = part_cross
        gram[1] = part_cross

        @pl.when(t == 0)
        def _():
            second_cross = dot_tn(merged, other[t].reshape(512, 128))

            @pl.when(core == 0)
            def _():
                gram_send[t, 1] = second_cross

            @pl.when(core == 1)
            def _():
                gram[1] = second_cross

        g_copy(t, 1).start()
        g_copy(t, 0).wait()
        gram[0] = part_gram + gram_recv[t, 0]
        cholesky_inverse(gram.at[0], linv)
        factor = linv[...]

        @pl.when(t < LEVELS - 1)
        def _():
            w_mine[t + 1] = dot_tn(factor, halves[t + 1])

        for step in range(LEVELS - 1):
            @pl.when(t == step)
            def _(step=step):
                w_copy(step, partners[step + 1]).start()

        g_copy(t, 1).wait()
        path[...] = dot_nn(factor, dot_nn(gram[1] + gram_recv[t, 1], before[...]))

        @pl.when((t == 4) & (core != x0))
        def _():
            swap_copy().start()
            swap_copy().wait()
            path[...] = swap[...]

        before[...] = dot_tn(factor, path[...])

        @pl.when(t < LEVELS - 1)
        def _():
            y_copy(t, (u_core, v)).wait()
            w_copy(t, (u_core, v)).wait()

        return carry

    lax.fori_loop(0, LEVELS, merge, 0)
    path_out[...] = path[...]
    root_out[...] = dot_nt(mine[LEVELS, y], linv[...])


def tree(far_left, sketch, keys):
    square = jax.ShapeDtypeStruct((128, 128), f32)
    vmem = pl.BlockSpec(memory_space=pltpu.VMEM)
    dma = pltpu.SemaphoreType.DMA
    return pl.pallas_call(
        tree_kernel,
        out_shape=(square, square),
        in_specs=[pl.BlockSpec(memory_space=pl.ANY), vmem, vmem],
        out_specs=(vmem, vmem),
        scratch_shapes=[
            pltpu.VMEM((LEVELS + 1, 4, 128, 128), f32),
            pltpu.VMEM((LEVELS + 1, 4, 128, 128), f32),
            pltpu.VMEM((LEVELS + 1, 128, 128), f32),
            pltpu.VMEM((LEVELS + 1, 128, 128), f32),
            pltpu.VMEM((LEVELS, 128, 128), f32),
            pltpu.VMEM((LEVELS, 2, 128, 128), f32),
            pltpu.VMEM((LEVELS, 2, 128, 128), f32),
            pltpu.VMEM((2, 128, 128), f32),
            pltpu.VMEM((128, 128), f32),
            pltpu.VMEM((128, 128), f32),
            pltpu.VMEM((128, 128), f32),
            pltpu.VMEM((128, 128), f32),
            dma, dma((2,)), dma((2,)),
            dma((LEVELS,)), dma((LEVELS,)), dma((LEVELS,)), dma((LEVELS,)),
            dma((LEVELS, 2)), dma((LEVELS, 2)), dma, dma,
        ],
        compiler_params=pltpu.CompilerParams(collective_id=0, has_side_effects=True, vmem_limit_bytes=32 * 2**20),
        cost_estimate=pl.CostEstimate(flops=10**10, bytes_accessed=2**20, transcendentals=0),
        name="tree",
    )(far_left.reshape(4, 2, 128, 128), sketch, keys)


def near_block(i, j, links, ext, near):
    where = []
    for s in range(6):
        e = links[i, 6 * j + s]
        down = (e * 11) // 32
        where.append((jnp.where(e < 9, i + down, 8), jnp.where(e < 9, j + e - 3 * down, 0)))
    lhs = jnp.concatenate([near[i, j, s] for s in range(6)], axis=1)
    rhs = jnp.concatenate([ext[a, b] for a, b in where], axis=0)
    summed = jnp.dot(lhs, rhs, preferred_element_type=f32)
    return (ext[i + 1, j + 1].astype(f32) + summed).astype(jnp.bfloat16)


def near_kernel(
    links, density, low, high, west, east, near_hbm, right_hbm, path, corrected, out_ref,
    ext, near, right, out, coef, sem, halo_sem, out_sem,
):
    bands = []
    for r in range(6):
        band = [
            pltpu.make_async_copy(density.at[r], ext.at[r + 1, 1:7], sem.at[r, 0]),
            pltpu.make_async_copy(near_hbm.at[r], near.at[r], sem.at[r, 1]),
            pltpu.make_async_copy(right_hbm.at[r], right.at[r], sem.at[r, 2]),
        ]
        for copy in band:
            copy.start()
        bands.append(band)
    halo = [
        pltpu.make_async_copy(low, ext.at[0, 1:7], halo_sem.at[0]),
        pltpu.make_async_copy(high, ext.at[7, 1:7], halo_sem.at[1]),
        pltpu.make_async_copy(west, ext.at[0:8, 0], halo_sem.at[2]),
        pltpu.make_async_copy(east, ext.at[0:8, 7], halo_sem.at[3]),
    ]
    for copy in halo:
        copy.start()
    ext[8, 0] = jnp.zeros((128, 768), jnp.bfloat16)
    coef[...] = jnp.zeros_like(coef)
    for copy in halo:
        copy.wait()
    for band in bands:
        for copy in band:
            copy.wait()

    def out_copy(i):
        return pltpu.make_async_copy(out.at[i], corrected.at[i], out_sem.at[i])

    def line(i, carry):
        def pair(m, inner):
            j = 2 * m
            done = []
            for q in range(2):
                block = near_block(i, j + q, links, ext, near)
                out[i, j + q] = block
                done.append(block)
            lhs = jnp.concatenate([right[i, j], right[i, j + 1]], axis=0)
            coef[...] += lax.dot_general(
                lhs, jnp.concatenate(done, axis=0), (((0,), (0,)), ((), ())), preferred_element_type=f32
            )
            return inner

        lax.fori_loop(0, 3, pair, 0)
        out_copy(i).start()
        return carry

    lax.fori_loop(0, 6, line, 0)
    out_ref[...] = lax.dot_general(coef[...], path[...], (((0,), (1,)), ((), ())), precision=highest, preferred_element_type=f32)
    for i in range(6):
        out_copy(i).wait()


def near_field(links, density, low, high, west, east, near_blocks, far_right, path):
    anywhere = pl.BlockSpec(memory_space=pl.ANY)
    vmem = pl.BlockSpec(memory_space=pltpu.VMEM)
    dma = pltpu.SemaphoreType.DMA
    return pl.pallas_call(
        near_kernel,
        out_shape=(jax.ShapeDtypeStruct((6, 6, 128, 768), jnp.bfloat16), jax.ShapeDtypeStruct((768, 128), f32)),
        in_specs=[pl.BlockSpec(memory_space=pltpu.SMEM)] + [anywhere] * 7 + [vmem],
        out_specs=(anywhere, vmem),
        scratch_shapes=[
            pltpu.VMEM((9, 8, 128, 768), jnp.bfloat16),
            pltpu.VMEM((6, 6, 6, 128, 128), jnp.bfloat16),
            pltpu.VMEM((6, 6, 128, 128), jnp.bfloat16),
            pltpu.VMEM((6, 6, 128, 768), jnp.bfloat16),
            pltpu.VMEM((128, 768), f32),
            dma((6, 3)), dma((4,)), dma((6,)),
        ],
        compiler_params=pltpu.CompilerParams(vmem_limit_bytes=48 * 2**20),
        name="near",
    )(links.reshape(6, 36), density, low, high, west, east, near_blocks, far_right, path)


def gather_kernel(term, root, out_ref, from_row, row_sum, from_col, row_send, row_recv, col_send, col_recv):
    u = lax.axis_index("pu")
    v = lax.axis_index("pv")
    barrier = pltpu.get_barrier_semaphore()
    for d in range(1, 16):
        pl.semaphore_signal(barrier, inc=1, device_id=(u, (v + d) % 16), device_id_type=MESH)
    for d in range(1, 8):
        pl.semaphore_signal(barrier, inc=1, device_id=((u + d) % 8, v), device_id_type=MESH)
    pl.semaphore_wait(barrier, 22)
    copies = []
    for d in range(1, 16):
        to = (v + d) % 16
        copy = pltpu.make_async_remote_copy(
            src_ref=term.at[to], dst_ref=from_row.at[d], send_sem=row_send.at[d], recv_sem=row_recv.at[d],
            device_id=(u, to), device_id_type=MESH,
        )
        copy.start()
        copies.append(copy)
    total = term[v]
    for d in range(1, 16):
        copies[d - 1].wait()
        total = total + from_row[d]
    row_sum[...] = total
    copies = []
    for d in range(1, 8):
        copy = pltpu.make_async_remote_copy(
            src_ref=row_sum, dst_ref=from_col.at[d], send_sem=col_send.at[d], recv_sem=col_recv.at[d],
            device_id=((u + d) % 8, v), device_id_type=MESH,
        )
        copy.start()
        copies.append(copy)
    for d in range(1, 8):
        copies[d - 1].wait()
        total = total + from_col[d]
    out_ref[...] = dot_nt(root[...], total)


def gathered(term, root):
    vmem = pl.BlockSpec(memory_space=pltpu.VMEM)
    dma = pltpu.SemaphoreType.DMA
    return pl.pallas_call(
        gather_kernel,
        out_shape=jax.ShapeDtypeStruct((128, 48), f32),
        in_specs=[vmem, vmem],
        out_specs=vmem,
        scratch_shapes=[
            pltpu.VMEM((16, 48, 128), f32), pltpu.VMEM((48, 128), f32), pltpu.VMEM((8, 48, 128), f32),
            dma((16,)), dma((16,)), dma((8,)), dma((8,)),
        ],
        compiler_params=pltpu.CompilerParams(collective_id=1, has_side_effects=True, vmem_limit_bytes=16 * 2**20),
        name="gather",
    )(term.reshape(16, 48, 128), root)


def from_sides(block, axis, dim):
    count = lax.axis_size(axis)
    forward = [(i, i + 1) for i in range(count - 1)]
    backward = [(target, source) for source, target in forward]
    low = lax.ppermute(lax.slice_in_dim(block, block.shape[dim] - 1, None, axis=dim), axis, forward)
    high = lax.ppermute(lax.slice_in_dim(block, 0, 1, axis=dim), axis, backward)
    return low, high


def per_device(density, near_blocks, neighbours, far_right, far_left, sketch, patch_order):
    low, high = from_sides(density, "pu", 0)
    edges = jnp.concatenate([low[:, ::5], density[:, ::5], high[:, ::5]], axis=0)
    west, east = from_sides(edges, "pv", 1)
    path, root = tree(far_left, sketch, patch_order.reshape(8, 16))
    corrected, term = near_field(
        neighbours, density, low[0], high[0], west[:, 0], east[:, 0], near_blocks, far_right, path
    )
    return (corrected, gathered(term, root))


def solution(mesh):
    in_specs = (
        P("pu", "pv", None, None),
        P("pu", "pv", None, None, None),
        P("pu", "pv", None),
        P("pu", "pv", None, None),
        P("pu", "pv", None, None),
        P(),
        P(),
    )
    out_specs = (P("pu", "pv", None, None), P("pu", "pv"))
    return jax.shard_map(
        per_device, mesh=mesh, in_specs=in_specs, out_specs=out_specs, check_vma=False
    )
```

```python
import functools

import jax
import jax.numpy as jnp
from jax import lax
from jax.experimental import pallas as pl
from jax.experimental.pallas import tpu as pltpu
from jax.sharding import PartitionSpec as P

MESH = pl.DeviceIdType.MESH
highest = lax.Precision.HIGHEST
f32 = jnp.float32
LEVELS = 7


def dot_nn(a, b):
    return lax.dot_general(a, b, (((1,), (0,)), ((), ())), precision=highest, preferred_element_type=f32)


def dot_tn(a, b):
    return lax.dot_general(a, b, (((0,), (0,)), ((), ())), precision=highest, preferred_element_type=f32)


def dot_nt(a, b):
    return lax.dot_general(a, b, (((1,), (1,)), ((), ())), precision=highest, preferred_element_type=f32)


def tile(x):
    return jnp.broadcast_to(x, (8, 128))


def cholesky_inverse(gram, out_ref):
    groups = 16
    row = lax.broadcasted_iota(jnp.int32, (8, 128), 0)
    lane = lax.broadcasted_iota(jnp.int32, (8, 128), 1)
    left = [gram[8 * g : 8 * g + 8, :] for g in range(groups)]
    right = [jnp.where(lane == row + 8 * g, 1.0, 0.0).astype(f32) for g in range(groups)]
    for b in range(groups):
        base = 8 * b
        last = b == groups - 1
        cols = [[tile(left[g][:, base + k : base + k + 1]) for k in range(8)] for g in range(b, groups)]
        d = [[tile(cols[0][k][i : i + 1, :]) for k in range(i + 1)] for i in range(8)]
        low = [[None] * 8 for _ in range(8)]
        inv = [[None] * 8 for _ in range(8)]
        for k in range(8):
            scale = lax.rsqrt(d[k][k])
            for i in range(k + 1, 8):
                low[i][k] = d[i][k] * scale
            for m in range(k + 1, 8):
                for i in range(m, 8):
                    d[i][m] = d[i][m] - low[i][k] * low[m][k]
            inv[k][k] = scale
            for j in range(k):
                s = low[k][j] * inv[j][j]
                for q in range(j + 1, k):
                    s = s + low[k][q] * inv[q][j]
                inv[k][j] = -(scale * s)

        def solved(panel):
            up = []
            for i in range(8):
                s = inv[i][0] * panel[0]
                for k in range(1, i + 1):
                    s = s + inv[i][k] * panel[k]
                up.append(s)
            return up

        def solved_again(up):
            full = []
            for k in range(8):
                s = inv[k][k] * up[k]
                for i in range(k + 1, 8):
                    s = s + inv[i][k] * up[i]
                full.append(s)
            return full

        up_right = solved([tile(right[b][k : k + 1, :]) for k in range(8)])
        for i in range(8):
            out_ref[base + i : base + i + 1, :] = up_right[i][0:1, :]
        if last:
            break
        full_left = solved_again(solved([tile(left[b][k : k + 1, :]) for k in range(8)]))
        full_right = solved_again(up_right)
        for g in range(b + 1, groups):
            c = cols[g - b]
            drop_left = c[0] * full_left[0]
            drop_right = c[0] * full_right[0]
            for k in range(1, 8):
                drop_left = drop_left + c[k] * full_left[k]
                drop_right = drop_right + c[k] * full_right[k]
            left[g] = left[g] - drop_left
            right[g] = right[g] - drop_right


def flip(index, bit):
    return index + bit - 2 * bit * ((index // bit) % 2)


def near_pair(i, cols, links, source, shift, near, right, out, coef):
    done = []
    for j in cols:
        where = []
        for s in range(6):
            e = links[i, 6 * j + s]
            down = (e * 11) // 32
            across = e - 3 * down
            where.append(
                (jnp.where(e < 9, i + down + shift - 1, 6 + 2 * shift), jnp.where(e < 9, j + across + shift - 1, 0))
            )
        lhs = jnp.concatenate([near[i, j, s] for s in range(6)], axis=1)
        rhs = jnp.concatenate([source[a, b] for a, b in where], axis=0)
        summed = jnp.dot(lhs, rhs, preferred_element_type=f32)
        block = (source[i + shift, j + shift].astype(f32) + summed).astype(jnp.bfloat16)
        out[i, j] = block
        done.append(block)
    lhs = jnp.concatenate([right[i, j] for j in cols], axis=0)
    coef[...] += lax.dot_general(
        lhs, jnp.concatenate(done, axis=0), (((0,), (0,)), ((), ())), preferred_element_type=f32
    )


def solver_kernel(
    links, density, near_hbm, right_hbm, leaf, sketch, keys, corrected, far_out,
    ext, inner, near, right, out, coef,
    mine, other, w_mine, w_other, halves, base, cross_send, cross_recv, cross, gram, linv, path, swap,
    term, from_row, row_sum, from_col,
    load_sem, out_sem, halo_send, halo_recv,
    leaf_local, leaf_send, leaf_recv, y_send, y_recv, w_send, w_recv, c_send, c_recv, g_send, g_recv, s_send, s_recv,
    row_send, row_recv, col_send, col_recv,
):
    u = lax.axis_index("pu")
    v = lax.axis_index("pv")
    core = u % 2
    y = u // 2
    x0 = v % 2
    u_core = flip(u, 1)
    v_next = flip(v, 1)
    partners = {1: (u, flip(v, 2)), 2: (u, flip(v, 4)), 3: (u, flip(v, 8)), 4: (u, v_next), 5: (flip(u, 2), v), 6: (flip(u, 4), v)}
    barrier = pltpu.get_barrier_semaphore()
    peers = list(partners.values()) + [(u_core, v), (u_core, v_next)]
    for du in (7, 0, 1):
        for dv in (15, 0, 1):
            if du or dv:
                peers.append(((u + du) % 8, (v + dv) % 16))
    for peer in peers:
        pl.semaphore_signal(barrier, inc=1, device_id=peer, device_id_type=MESH)
    loads = [
        pltpu.make_async_copy(near_hbm, near, load_sem.at[0]),
        pltpu.make_async_copy(density, inner.at[0:6], load_sem.at[1]),
        pltpu.make_async_copy(right_hbm, right, load_sem.at[2]),
        pltpu.make_async_copy(density, ext.at[1:7, 1:7], load_sem.at[3]),
    ]
    pl.semaphore_wait(barrier, len(peers))

    def leaf_copy(part, slot_ref, to, slot):
        return pltpu.make_async_remote_copy(
            src_ref=leaf.at[:, part], dst_ref=slot_ref.at[0], send_sem=leaf_send.at[part],
            recv_sem=leaf_recv.at[slot], device_id=to, device_id_type=MESH,
        )

    slots = (mine, other)
    for c in range(2):
        for x in range(2):
            @pl.when((core == c) & (x0 == x))
            def _(c=c, x=x):
                if c == x:
                    leaf_copy(1 - c, slots[x], (u_core, v), x).start()
                    pltpu.make_async_copy(leaf.at[:, c], slots[x].at[0], leaf_local).start()
                else:
                    leaf_copy(c, slots[x], (u, v_next), x).start()
                    leaf_copy(1 - c, slots[x], (u_core, v_next), x).start()
    for copy in loads:
        copy.start()

    up, down, west, east = u > 0, u < 7, v > 0, v < 15
    halo = [
        (density.at[0], ext.at[7, 1:7], (u - 1, v), up, down),
        (density.at[5], ext.at[0, 1:7], (u + 1, v), down, up),
    ]
    for r in range(3):
        rows = slice(2 * r, 2 * r + 2)
        to_rows = slice(2 * r + 1, 2 * r + 3)
        halo.append((density.at[rows, 0], ext.at[to_rows, 7], (u, v - 1), west, east))
        halo.append((density.at[rows, 5], ext.at[to_rows, 0], (u, v + 1), east, west))
    halo += [
        (density.at[0, 0], ext.at[7, 7], (u - 1, v - 1), up & west, down & east),
        (density.at[5, 5], ext.at[0, 0], (u + 1, v + 1), down & east, up & west),
        (density.at[0, 5], ext.at[7, 0], (u - 1, v + 1), up & east, down & west),
        (density.at[5, 0], ext.at[0, 7], (u + 1, v - 1), down & west, up & east),
    ]

    def halo_copy(n):
        source, target, to, _, _ = halo[n]
        return pltpu.make_async_remote_copy(
            src_ref=source, dst_ref=target, send_sem=halo_send.at[n], recv_sem=halo_recv.at[n],
            device_id=to, device_id_type=MESH,
        )

    def halo_start(numbers):
        for n in numbers:
            @pl.when(halo[n][3])
            def _(n=n):
                halo_copy(n).start()

    def halo_wait():
        for n in range(len(halo)):
            @pl.when(halo[n][3])
            def _(n=n):
                halo_copy(n).wait_send()

            @pl.when(halo[n][4])
            def _(n=n):
                halo_copy(n).wait_recv()

    halo_start((0, 1, 2, 3))
    zero = jnp.zeros((128, 768), jnp.bfloat16)
    ext[8, 0] = zero
    inner[6, 0] = zero
    for edge, cells in (
        (u == 0, [(0, n) for n in range(8)]),
        (u == 7, [(7, n) for n in range(8)]),
        (v == 0, [(n, 0) for n in range(8)]),
        (v == 15, [(n, 7) for n in range(8)]),
    ):
        @pl.when(edge)
        def _(cells=cells):
            for a, b in cells:
                ext[a, b] = zero
    coef[...] = jnp.zeros_like(coef)

    key = keys[...]
    rows = lax.broadcasted_iota(jnp.int32, (8, 16), 0)
    cols = lax.broadcasted_iota(jnp.int32, (8, 16), 1)
    host_row = 2 * y + x0

    def least(mask):
        return jnp.min(jnp.min(jnp.where(mask, key, 1 << 20), axis=1, keepdims=True), axis=0, keepdims=True)

    here = rows == host_row
    even = v - x0
    pairs = [(here & (cols == even), here & (cols == even + 1))]
    for bit in (2, 4, 8):
        pairs.append((here & (cols // bit == v // bit), here & (cols // bit == flip(v, bit) // bit)))
    pairs.append((here, rows == 2 * y + 1 - x0))
    for bit in (2, 4):
        pairs.append((rows // bit == u // bit, rows // bit == flip(u, bit) // bit))
    first = sketch[0:128, :]
    second = sketch[128:256, :]
    for t, (own, sibling) in enumerate(pairs):
        leads = jnp.broadcast_to((least(own) < least(sibling)).astype(f32), (128, 128)) > 0.5
        halves[t] = jnp.where(leads, first, second)
        if t == 0:
            w_mine[0] = halves[0]
            w_other[0] = jnp.where(leads, second, first)
    base[...] = dot_tn(sketch[...], sketch[...])

    def inner_pairs(low, high):
        def step(n, carry):
            j = 1 + 2 * (n % 2)
            near_pair(1 + n // 2, (j, j + 1), links, inner, 0, near, right, out, coef)
            return carry

        lax.fori_loop(low, high, step, 0)

    def edge_row(i):
        def step(n, carry):
            near_pair(i, (2 * n, 2 * n + 1), links, ext, 1, near, right, out, coef)
            return carry

        lax.fori_loop(0, 3, step, 0)

    def edge_cols(low, high):
        def step(i, carry):
            near_pair(i, (0, 5), links, ext, 1, near, right, out, coef)
            return carry

        lax.fori_loop(low, high, step, 0)

    for copy in loads:
        copy.wait()
    inner_pairs(0, 3)

    for c in range(2):
        for x in range(2):
            @pl.when((core == c) & (x0 == x))
            def _(c=c, x=x):
                if c == x:
                    pltpu.make_async_copy(leaf.at[:, c], slots[x].at[0], leaf_local).wait()
                    leaf_copy(1 - c, slots[x], (u_core, v), x).wait_send()
                    leaf_copy(0, slots[1 - x], (u_core, v), 1 - x).wait_recv()
                else:
                    for part in range(2):
                        leaf_copy(part, slots[x], (u_core, v), x).wait_send()
                    for slot in range(2):
                        leaf_copy(0, slots[slot], (u_core, v), slot).wait_recv()

    def y_copy(t, to):
        return pltpu.make_async_remote_copy(
            src_ref=mine.at[t + 1], dst_ref=other.at[t + 1], send_sem=y_send.at[t], recv_sem=y_recv.at[t],
            device_id=to, device_id_type=MESH,
        )

    def w_copy(t, to):
        return pltpu.make_async_remote_copy(
            src_ref=w_mine.at[t + 1], dst_ref=w_other.at[t + 1], send_sem=w_send.at[t], recv_sem=w_recv.at[t],
            device_id=to, device_id_type=MESH,
        )

    def cross_copy(t):
        return pltpu.make_async_remote_copy(
            src_ref=cross_send.at[t], dst_ref=cross_recv.at[t], send_sem=c_send.at[t], recv_sem=c_recv.at[t],
            device_id=(u_core, v), device_id_type=MESH,
        )

    def leaf_gram_copy(kind):
        return pltpu.make_async_remote_copy(
            src_ref=cross_send.at[LEVELS + kind], dst_ref=cross_recv.at[LEVELS + kind], send_sem=g_send.at[kind],
            recv_sem=g_recv.at[kind], device_id=(u_core, v), device_id_type=MESH,
        )

    def swap_copy():
        return pltpu.make_async_remote_copy(
            src_ref=path, dst_ref=swap, send_sem=s_send, recv_sem=s_recv,
            device_id=(u_core, v_next), device_id_type=MESH,
        )

    def row_copy(d):
        to = (v + d) % 16
        return pltpu.make_async_remote_copy(
            src_ref=term.at[to], dst_ref=from_row.at[d], send_sem=row_send.at[d], recv_sem=row_recv.at[d],
            device_id=(u, to), device_id_type=MESH,
        )

    out_copies = [
        pltpu.make_async_copy(out.at[1:5, 1:5], corrected.at[1:5, 1:5], out_sem.at[0]),
        pltpu.make_async_copy(out.at[0], corrected.at[0], out_sem.at[1]),
        pltpu.make_async_copy(out.at[5], corrected.at[5], out_sem.at[2]),
        pltpu.make_async_copy(out.at[1:5, 0], corrected.at[1:5, 0], out_sem.at[3]),
        pltpu.make_async_copy(out.at[1:5, 5], corrected.at[1:5, 5], out_sem.at[4]),
    ]

    def merge(t, carry):
        for r in range(4):
            mine[t + 1, r] = dot_nn(mine[t, r], w_mine[t]) + dot_nn(other[t, r], w_other[t])
        for step in range(LEVELS - 1):
            @pl.when(t == step)
            def _(step=step):
                y_copy(step, partners[step + 1]).start()
                if step == 1:
                    halo_start((4, 5, 8, 9))
                if step == 2:
                    halo_start((6, 7, 10, 11))

        @pl.when(t == 0)
        def _():
            merged = mine[1].reshape(512, 128)
            part = dot_tn(merged, merged)
            cross_send[LEVELS] = part
            leaf_gram_copy(0).start()
            ours = dot_tn(merged, mine[0].reshape(512, 128))
            theirs = dot_tn(merged, other[0].reshape(512, 128))
            cross_send[LEVELS + 1] = jnp.where(core == 0, theirs, ours)
            leaf_gram_copy(1).start()
            leaf_gram_copy(0).wait()
            gram[...] = part + cross_recv[LEVELS]
            leaf_gram_copy(1).wait()
            path[...] = jnp.where(core == 0, ours, theirs) + cross_recv[LEVELS + 1]

        @pl.when(t > 0)
        def _():
            mixed = dot_nn(cross[...], w_other[t])
            half = dot_tn(w_mine[t], mixed)
            gram[...] = base[...] + half + half.T
            path[...] = dot_tn(halves[t], path[...]) + dot_tn(mixed, dot_tn(linv[...], path[...]))

        cholesky_inverse(gram, linv)

        @pl.when(t < LEVELS - 1)
        def _():
            w_mine[t + 1] = dot_tn(linv[...], halves[t + 1])

        for step in range(LEVELS - 1):
            @pl.when(t == step)
            def _(step=step):
                w_copy(step, partners[step + 1]).start()

        path[...] = dot_nn(linv[...], path[...])

        @pl.when((t == 4) & (core != x0))
        def _():
            swap_copy().start()
            swap_copy().wait()
            path[...] = swap[...]

        @pl.when(t == 0)
        def _():
            inner_pairs(3, 8)
            out_copies[0].start()

        @pl.when(t == 3)
        def _():
            halo_wait()
            edge_row(0)
            out_copies[1].start()

        @pl.when(t == 4)
        def _():
            edge_row(5)
            out_copies[2].start()

        @pl.when(t == 5)
        def _():
            edge_cols(1, 5)
            out_copies[3].start()
            out_copies[4].start()
            products = lax.dot_general(
                coef[...], path[...], (((0,), (1,)), ((), ())), precision=highest, preferred_element_type=f32
            )
            term[...] = products.reshape(16, 48, 128)
            for d in range(1, 16):
                row_copy(d).start()
            path[...] = diag_matrix()

        @pl.when(t < LEVELS - 1)
        def _():
            y_copy(t, (u_core, v)).wait()
            part = dot_tn(mine[t + 1].reshape(512, 128), other[t + 1].reshape(512, 128))
            cross_send[t] = part
            cross_copy(t).start()
            cross_copy(t).wait()
            cross[...] = part + cross_recv[t]
            w_copy(t, (u_core, v)).wait()

        return carry

    def diag_matrix():
        down_iota = lax.broadcasted_iota(jnp.int32, (128, 128), 0)
        return jnp.where(down_iota == lax.broadcasted_iota(jnp.int32, (128, 128), 1), 1.0, 0.0).astype(f32)

    lax.fori_loop(0, LEVELS, merge, 0)
    total = term[v]
    for d in range(1, 16):
        row_copy(d).wait()
        total = total + from_row[d]
    total = dot_nt(total, path[...])
    row_sum[...] = total
    copies = []
    for d in range(1, 8):
        copy = pltpu.make_async_remote_copy(
            src_ref=row_sum, dst_ref=from_col.at[d], send_sem=col_send.at[d], recv_sem=col_recv.at[d],
            device_id=((u + d) % 8, v), device_id_type=MESH,
        )
        copy.start()
        copies.append(copy)
    root = dot_nt(mine[LEVELS, y], linv[...])
    for copy in out_copies:
        copy.wait()
    for d in range(1, 8):
        copies[d - 1].wait()
        total = total + from_col[d]
    far_out[...] = dot_nt(root, total)


def solve(links, density, near_blocks, far_right, far_left, sketch, keys):
    anywhere = pl.BlockSpec(memory_space=pl.ANY)
    vmem = pl.BlockSpec(memory_space=pltpu.VMEM)
    dma = pltpu.SemaphoreType.DMA
    bf16 = jnp.bfloat16
    return pl.pallas_call(
        solver_kernel,
        out_shape=(jax.ShapeDtypeStruct((6, 6, 128, 768), bf16), jax.ShapeDtypeStruct((128, 48), f32)),
        in_specs=[pl.BlockSpec(memory_space=pltpu.SMEM)] + [anywhere] * 4 + [vmem, vmem],
        out_specs=(anywhere, vmem),
        scratch_shapes=[
            pltpu.VMEM((9, 8, 128, 768), bf16),
            pltpu.VMEM((7, 6, 128, 768), bf16),
            pltpu.VMEM((6, 6, 6, 128, 128), bf16),
            pltpu.VMEM((6, 6, 128, 128), bf16),
            pltpu.VMEM((6, 6, 128, 768), bf16),
            pltpu.VMEM((128, 768), f32),
            pltpu.VMEM((LEVELS + 1, 4, 128, 128), f32),
            pltpu.VMEM((LEVELS + 1, 4, 128, 128), f32),
            pltpu.VMEM((LEVELS + 1, 128, 128), f32),
            pltpu.VMEM((LEVELS + 1, 128, 128), f32),
            pltpu.VMEM((LEVELS, 128, 128), f32),
            pltpu.VMEM((128, 128), f32),
            pltpu.VMEM((LEVELS + 2, 128, 128), f32),
            pltpu.VMEM((LEVELS + 2, 128, 128), f32),
            pltpu.VMEM((128, 128), f32),
            pltpu.VMEM((128, 128), f32),
            pltpu.VMEM((128, 128), f32),
            pltpu.VMEM((128, 128), f32),
            pltpu.VMEM((128, 128), f32),
            pltpu.VMEM((16, 48, 128), f32),
            pltpu.VMEM((16, 48, 128), f32),
            pltpu.VMEM((48, 128), f32),
            pltpu.VMEM((8, 48, 128), f32),
            dma((4,)), dma((5,)), dma((12,)), dma((12,)),
            dma, dma((2,)), dma((2,)),
            dma((LEVELS,)), dma((LEVELS,)), dma((LEVELS,)), dma((LEVELS,)),
            dma((LEVELS,)), dma((LEVELS,)), dma((2,)), dma((2,)), dma, dma,
            dma((16,)), dma((16,)), dma((8,)), dma((8,)),
        ],
        compiler_params=pltpu.CompilerParams(collective_id=0, has_side_effects=True, vmem_limit_bytes=60 * 2**20),
        cost_estimate=pl.CostEstimate(flops=10**10, bytes_accessed=2**25, transcendentals=0),
        name="solver",
    )(links.reshape(6, 36), density, near_blocks, far_right, far_left.reshape(4, 2, 128, 128), sketch, keys)


def copy_kernel(source, target, held, in_sem, out_sem):
    reads = [pltpu.make_async_copy(source.at[i], held.at[i], in_sem.at[i]) for i in range(6)]
    writes = [pltpu.make_async_copy(held.at[i], target.at[i], out_sem.at[i]) for i in range(6)]
    for copy in reads:
        copy.start()
    for read, write in zip(reads, writes):
        read.wait()
        write.start()
    for copy in writes:
        copy.wait()


def copied(value):
    anywhere = pl.BlockSpec(memory_space=pl.ANY)
    return pl.pallas_call(
        copy_kernel,
        out_shape=jax.ShapeDtypeStruct(value.shape, value.dtype),
        in_specs=[anywhere],
        out_specs=anywhere,
        scratch_shapes=[
            pltpu.VMEM(value.shape, value.dtype), pltpu.SemaphoreType.DMA((6,)), pltpu.SemaphoreType.DMA((6,)),
        ],
        compiler_params=pltpu.CompilerParams(vmem_limit_bytes=16 * 2**20),
        name="copy_out",
    )(value)


def per_device(density, near_blocks, neighbours, far_right, far_left, sketch, patch_order):
    corrected, far_field = solve(
        neighbours, density, near_blocks, far_right, far_left, sketch, patch_order.reshape(8, 16)
    )
    return (copied(corrected), far_field)


def solution(mesh):
    in_specs = (
        P("pu", "pv", None, None),
        P("pu", "pv", None, None, None),
        P("pu", "pv", None),
        P("pu", "pv", None, None),
        P("pu", "pv", None, None),
        P(),
        P(),
    )
    out_specs = (P("pu", "pv", None, None), P("pu", "pv"))
    return jax.shard_map(
        per_device, mesh=mesh, in_specs=in_specs, out_specs=out_specs, check_vma=False
    )
```

```python
import functools

import jax
import jax.numpy as jnp
from jax import lax
from jax.experimental import pallas as pl
from jax.experimental.pallas import tpu as pltpu
from jax.sharding import PartitionSpec as P

MESH = pl.DeviceIdType.MESH
highest = lax.Precision.HIGHEST
f32 = jnp.float32
LEVELS = 7
INNER = (0, 3, 6, 9, 12)


def dot_nn(a, b):
    return lax.dot_general(a, b, (((1,), (0,)), ((), ())), precision=highest, preferred_element_type=f32)


def dot_tn(a, b):
    return lax.dot_general(a, b, (((0,), (0,)), ((), ())), precision=highest, preferred_element_type=f32)


def dot_nt(a, b):
    return lax.dot_general(a, b, (((1,), (1,)), ((), ())), precision=highest, preferred_element_type=f32)


def tile(x):
    return jnp.broadcast_to(x, (8, 128))


def tree_sum(terms):
    while len(terms) > 1:
        terms = [terms[i] + terms[i + 1] if i + 1 < len(terms) else terms[i] for i in range(0, len(terms), 2)]
    return terms[0]


def cholesky_inverse(gram, out_ref, panels):
    groups = 16
    row = lax.broadcasted_iota(jnp.int32, (8, 128), 0)
    lane = lax.broadcasted_iota(jnp.int32, (8, 128), 1)
    left = [gram[8 * g : 8 * g + 8, :] for g in range(groups)]
    right = [jnp.where(lane == row + 8 * g, 1.0, 0.0).astype(f32) for g in range(groups)]
    for b in range(groups):
        base = 8 * b
        last = b == groups - 1
        cols = [[tile(left[g][:, base + k : base + k + 1]) for k in range(8)] for g in range(b, groups)]
        for k in range(8):
            panels[b, k] = cols[0][k]
        panels[b, 8] = left[b]
        panels[b, 9] = right[b]
        d = [[tile(panels[b, k, i : i + 1, :]) for k in range(i + 1)] for i in range(8)]
        low = [[None] * 8 for _ in range(8)]
        inv = [[None] * 8 for _ in range(8)]
        for k in range(0, 8, 2):
            p, q, r = d[k][k], d[k + 1][k], d[k + 1][k + 1]
            scale = lax.rsqrt(p)
            second = lax.rsqrt(p * r - q * q)
            both = scale * second
            low[k + 1][k] = q * scale
            for i in range(k + 2, 8):
                low[i][k] = d[i][k] * scale
                low[i][k + 1] = (p * d[i][k + 1] - d[i][k] * q) * both
            for m in range(k + 2, 8):
                for i in range(m, 8):
                    d[i][m] = d[i][m] - (low[i][k] * low[m][k] + low[i][k + 1] * low[m][k + 1])
            for n, pivot in ((k, scale), (k + 1, p * both)):
                inv[n][n] = pivot
                for j in range(n):
                    inv[n][j] = -(pivot * tree_sum([low[n][h] * inv[h][j] for h in range(j, n)]))

        def solved(panel):
            return [tree_sum([inv[i][k] * panel[k] for k in range(i + 1)]) for i in range(8)]

        def solved_again(up):
            return [tree_sum([inv[i][k] * up[i] for i in range(k, 8)]) for k in range(8)]

        up_right = solved([tile(panels[b, 9, k : k + 1, :]) for k in range(8)])
        for i in range(8):
            out_ref[base + i : base + i + 1, :] = up_right[i][0:1, :]
        if last:
            break
        full_left = solved_again(solved([tile(panels[b, 8, k : k + 1, :]) for k in range(8)]))
        full_right = solved_again(up_right)
        for g in range(b + 1, groups):
            c = cols[g - b]
            left[g] = left[g] - tree_sum([c[k] * full_left[k] for k in range(8)])
            right[g] = right[g] - tree_sum([c[k] * full_right[k] for k in range(8)])


def flip(index, bit):
    return index + bit - 2 * bit * ((index // bit) % 2)


def near_pair(i, cols, places, links, source, near, right, out, coef):
    done = []
    for j, place in zip(cols, places):
        where = []
        for s in range(6):
            e = links[i, j, s]
            down = (e * 11) // 32
            across = e - 3 * down
            where.append((jnp.where(e < 9, i + down, 8), jnp.where(e < 9, place + across - 1, 0)))
        lhs = jnp.concatenate([near[i, j, s] for s in range(6)], axis=1)
        rhs = jnp.concatenate([source[a, b] for a, b in where], axis=0)
        summed = jnp.dot(lhs, rhs, preferred_element_type=f32)
        block = (source[i + 1, place].astype(f32) + summed).astype(jnp.bfloat16)
        out[i, j] = block
        done.append(block)
    lhs = jnp.concatenate([right[i, j] for j in cols], axis=0)
    coef[...] += lax.dot_general(
        lhs, jnp.concatenate(done, axis=0), (((0,), (0,)), ((), ())), preferred_element_type=f32
    )


def split(value):
    high = value.astype(jnp.bfloat16)
    return high, (value - high.astype(f32)).astype(jnp.bfloat16)


def dot_sum(a, b, wide):
    a_high, a_low = split(a)
    b_high, b_low = split(b)
    return jnp.dot(
        jnp.concatenate([a_high, b_high, a_high, b_high, a_low, b_low], axis=1), wide, preferred_element_type=f32
    )


def widened(a, b):
    a_high, a_low = split(a)
    b_high, b_low = split(b)
    return jnp.concatenate([a_high, b_high, a_low, b_low, a_high, b_high], axis=0)


def solver_kernel(
    links, density, near_hbm, right_hbm, leaf, sketch, keys, corrected, far_out,
    ext, inner, near, right, out, coef,
    mine, other, w_mine, w_other, halves, base, cross_send, cross_recv, cross, gram, mixed, panels, linv, path, swap,
    term, from_row, row_sum, from_col,
    load_sem, out_sem, halo_send, halo_recv,
    leaf_local, leaf_send, leaf_recv, y_send, y_recv, w_send, w_recv, c_send, c_recv, g_send, g_recv, s_send, s_recv,
    row_send, row_recv, col_send, col_recv,
):
    u = lax.axis_index("pu")
    v = lax.axis_index("pv")
    core = u % 2
    y = u // 2
    x0 = v % 2
    u_core = flip(u, 1)
    v_next = flip(v, 1)
    partners = {1: (u, flip(v, 2)), 2: (u, flip(v, 4)), 3: (u, flip(v, 8)), 4: (u, v_next), 5: (flip(u, 2), v), 6: (flip(u, 4), v)}
    barrier = pltpu.get_barrier_semaphore()
    peers = list(partners.values()) + [(u_core, v), (u_core, v_next)]
    for du in (7, 0, 1):
        for dv in (15, 0, 1):
            if du or dv:
                peers.append(((u + du) % 8, (v + dv) % 16))
    for peer in peers:
        pl.semaphore_signal(barrier, inc=1, device_id=peer, device_id_type=MESH)
    loads = [
        pltpu.make_async_copy(near_hbm, near, load_sem.at[0]),
        pltpu.make_async_copy(density, inner.at[1:7], load_sem.at[1]),
        pltpu.make_async_copy(right_hbm, right, load_sem.at[2]),
        pltpu.make_async_copy(density.at[:, 0:2], ext.at[1:7, 1:3], load_sem.at[3]),
        pltpu.make_async_copy(density.at[:, 4:6], ext.at[1:7, 3:5], load_sem.at[4]),
    ]
    for copy in loads:
        copy.start()
    key = keys[...]
    patch = lax.broadcasted_iota(jnp.int32, (1, 128), 1)
    rows = patch // 16
    cols = patch % 16
    host_row = 2 * y + x0

    def least(mask):
        return jnp.min(jnp.where(mask, key, 1 << 20), axis=1, keepdims=True)

    here = rows == host_row
    even = v - x0
    pairs = [(here & (cols == even), here & (cols == even + 1))]
    for bit in (2, 4, 8):
        pairs.append((here & (cols // bit == v // bit), here & (cols // bit == flip(v, bit) // bit)))
    pairs.append((here, rows == 2 * y + 1 - x0))
    for bit in (2, 4):
        pairs.append((rows // bit == u // bit, rows // bit == flip(u, bit) // bit))
    first = sketch[0:128, :]
    second = sketch[128:256, :]
    for t, (own, sibling) in enumerate(pairs):
        leads = jnp.broadcast_to((least(own) < least(sibling)).astype(f32), (128, 128)) > 0.5
        halves[t] = jnp.where(leads, first, second)
        if t == 0:
            w_mine[0] = halves[0]
            w_other[0] = jnp.where(leads, second, first)
    base[...] = dot_tn(sketch[...], sketch[...])
    pl.semaphore_wait(barrier, len(peers))

    def leaf_copy(part, slot_ref, to, slot):
        return pltpu.make_async_remote_copy(
            src_ref=leaf.at[:, part], dst_ref=slot_ref.at[0], send_sem=leaf_send.at[part],
            recv_sem=leaf_recv.at[slot], device_id=to, device_id_type=MESH,
        )

    slots = (mine, other)
    for c in range(2):
        for x in range(2):
            @pl.when((core == c) & (x0 == x))
            def _(c=c, x=x):
                if c == x:
                    leaf_copy(1 - c, slots[x], (u_core, v), x).start()
                    pltpu.make_async_copy(leaf.at[:, c], slots[x].at[0], leaf_local).start()
                else:
                    leaf_copy(c, slots[x], (u, v_next), x).start()
                    leaf_copy(1 - c, slots[x], (u_core, v_next), x).start()
    up, down, west, east = u > 0, u < 7, v > 0, v < 15
    turn_west, turn_east = v % 4 == 0, v % 4 == 3
    halo = [
        (density.at[0], inner.at[7], (u - 1, v), up, down, None),
        (density.at[5], inner.at[0], (u + 1, v), down, up, None),
    ]
    for r in range(3):
        span = slice(2 * r, 2 * r + 2)
        to_span = slice(2 * r + 1, 2 * r + 3)
        halo.append((density.at[span, 0], ext.at[to_span, 5], (u, v - 1), west, east, turn_west))
        halo.append((density.at[span, 5], ext.at[to_span, 0], (u, v + 1), east, west, turn_east))
    halo += [
        (density.at[0, 0], ext.at[7, 5], (u - 1, v - 1), up & west, down & east, turn_west),
        (density.at[5, 5], ext.at[0, 0], (u + 1, v + 1), down & east, up & west, turn_east),
        (density.at[0, 5], ext.at[7, 0], (u - 1, v + 1), up & east, down & west, turn_east),
        (density.at[5, 0], ext.at[0, 5], (u + 1, v - 1), down & west, up & east, turn_west),
    ]

    def halo_copy(n):
        source, target, to = halo[n][:3]
        return pltpu.make_async_remote_copy(
            src_ref=source, dst_ref=target, send_sem=halo_send.at[n], recv_sem=halo_recv.at[n],
            device_id=to, device_id_type=MESH,
        )

    def halo_start(numbers, only=None):
        for n in numbers:
            due = halo[n][3]
            if only is not None:
                due = due & only

            @pl.when(due)
            def _(n=n):
                halo_copy(n).start()

    def halo_wait(numbers):
        for n in numbers:
            @pl.when(halo[n][3])
            def _(n=n):
                halo_copy(n).wait_send()

            @pl.when(halo[n][4])
            def _(n=n):
                halo_copy(n).wait_recv()

    even_v, odd_v = x0 == 0, x0 == 1
    halo_start((0, 1))
    halo_start((2,), even_v)
    halo_start((3,), odd_v)
    halo_start((4,), turn_west)
    halo_start((5,), turn_east)
    zero = jnp.zeros((128, 768), jnp.bfloat16)
    ext[8, 0] = zero
    inner[8, 0] = zero
    for edge, target, cells in (
        (u == 0, inner, [(0, n) for n in range(6)]),
        (u == 7, inner, [(7, n) for n in range(6)]),
        (u == 0, ext, [(0, 0), (0, 5)]),
        (u == 7, ext, [(7, 0), (7, 5)]),
        (v == 0, ext, [(n, 0) for n in range(8)]),
        (v == 15, ext, [(n, 5) for n in range(8)]),
    ):
        @pl.when(edge)
        def _(target=target, cells=cells):
            for a, b in cells:
                target[a, b] = zero
    coef[...] = jnp.zeros_like(coef)

    def inner_pairs(low, high):
        def step(n, carry):
            j = 1 + 2 * (n % 2)
            near_pair(n // 2, (j, j + 1), (j, j + 1), links, inner, near, right, out, coef)
            return carry

        lax.fori_loop(low, high, step, 0)

    def side_pairs(low, high):
        def step(i, carry):
            near_pair(i, (0, 5), (1, 4), links, ext, near, right, out, coef)
            return carry

        lax.fori_loop(low, high, step, 0)

    for c in range(2):
        for x in range(2):
            @pl.when((core == c) & (x0 == x))
            def _(c=c, x=x):
                if c == x:
                    pltpu.make_async_copy(leaf.at[:, c], slots[x].at[0], leaf_local).wait()
                    leaf_copy(1 - c, slots[x], (u_core, v), x).wait_send()
                    leaf_copy(0, slots[1 - x], (u_core, v), 1 - x).wait_recv()
                else:
                    for part in range(2):
                        leaf_copy(part, slots[x], (u_core, v), x).wait_send()
                    for slot in range(2):
                        leaf_copy(0, slots[slot], (u_core, v), slot).wait_recv()

    halo_start((2,), odd_v)
    halo_start((3,), even_v)
    straight_west, straight_east = jnp.logical_not(turn_west), jnp.logical_not(turn_east)

    def y_copy(t, part, to):
        span = slice(2 * part, 2 * part + 2)
        return pltpu.make_async_remote_copy(
            src_ref=mine.at[t + 1, span], dst_ref=other.at[t + 1, span],
            send_sem=y_send.at[t, part], recv_sem=y_recv.at[t, part],
            device_id=to, device_id_type=MESH,
        )

    def w_copy(t, to):
        return pltpu.make_async_remote_copy(
            src_ref=w_mine.at[t + 1], dst_ref=w_other.at[t + 1], send_sem=w_send.at[t], recv_sem=w_recv.at[t],
            device_id=to, device_id_type=MESH,
        )

    def cross_copy(t):
        return pltpu.make_async_remote_copy(
            src_ref=cross_send.at[t], dst_ref=cross_recv.at[t], send_sem=c_send.at[t], recv_sem=c_recv.at[t],
            device_id=(u_core, v), device_id_type=MESH,
        )

    def leaf_gram_copy(kind):
        return pltpu.make_async_remote_copy(
            src_ref=cross_send.at[LEVELS + kind], dst_ref=cross_recv.at[LEVELS + kind], send_sem=g_send.at[kind],
            recv_sem=g_recv.at[kind], device_id=(u_core, v), device_id_type=MESH,
        )

    def swap_copy():
        return pltpu.make_async_remote_copy(
            src_ref=path, dst_ref=swap, send_sem=s_send, recv_sem=s_recv,
            device_id=(u_core, v_next), device_id_type=MESH,
        )

    def row_copy(d):
        to = (v + d) % 16
        return pltpu.make_async_remote_copy(
            src_ref=term.at[to], dst_ref=from_row.at[d], send_sem=row_send.at[d], recv_sem=row_recv.at[d],
            device_id=(u, to), device_id_type=MESH,
        )

    out_copies = [
        pltpu.make_async_copy(out.at[:, 1:5], corrected.at[:, 1:5], out_sem.at[0]),
        pltpu.make_async_copy(out.at[:, 0], corrected.at[:, 0], out_sem.at[1]),
        pltpu.make_async_copy(out.at[:, 5], corrected.at[:, 5], out_sem.at[2]),
    ]

    def merge(t, carry):
        wide = widened(w_mine[t], w_other[t])
        for part in range(2):
            span = slice(2 * part, 2 * part + 2)
            both = dot_sum(mine[t, span].reshape(256, 128), other[t, span].reshape(256, 128), wide)
            mine[t + 1, span] = both.reshape(2, 128, 128)
            for step in range(LEVELS - 1):
                @pl.when(t == step)
                def _(step=step, part=part):
                    y_copy(step, part, partners[step + 1]).start()

        @pl.when(t == 1)
        def _():
            halo_start((4, 8), straight_west)
            halo_start((5, 9), straight_east)

        @pl.when(t == 2)
        def _():
            halo_start((6, 11), straight_west)
            halo_start((7, 10), straight_east)

        @pl.when(t == 3)
        def _():
            halo_start((6, 8, 11), turn_west)
            halo_start((7, 9, 10), turn_east)

        @pl.when(t == 0)
        def _():
            merged = mine[1].reshape(512, 128)
            part = dot_tn(merged, merged)
            cross_send[LEVELS] = part
            leaf_gram_copy(0).start()
            ours = dot_tn(merged, mine[0].reshape(512, 128))
            theirs = dot_tn(merged, other[0].reshape(512, 128))
            cross_send[LEVELS + 1] = jnp.where(core == 0, theirs, ours)
            leaf_gram_copy(1).start()
            leaf_gram_copy(0).wait()
            gram[...] = part + cross_recv[LEVELS]
            leaf_gram_copy(1).wait()
            path[...] = jnp.where(core == 0, ours, theirs) + cross_recv[LEVELS + 1]

        @pl.when(t > 0)
        def _():
            mixed[...] = dot_nn(cross[...], w_other[t])
            half = dot_tn(w_mine[t], mixed[...])
            gram[...] = base[...] + half + half.T

        cholesky_inverse(gram, linv.at[t], panels)

        @pl.when(t < LEVELS - 1)
        def _():
            w_mine[t + 1] = dot_tn(linv[t], halves[t + 1])

        for step in range(LEVELS - 1):
            @pl.when(t == step)
            def _(step=step):
                w_copy(step, partners[step + 1]).start()

        @pl.when(t < LEVELS - 1)
        def _():
            y_copy(t, 0, (u_core, v)).wait()
            part = dot_tn(mine[t + 1, 0:2].reshape(256, 128), other[t + 1, 0:2].reshape(256, 128))
            y_copy(t, 1, (u_core, v)).wait()
            part = part + dot_tn(mine[t + 1, 2:4].reshape(256, 128), other[t + 1, 2:4].reshape(256, 128))
            cross_send[t] = part
            cross_copy(t).start()

        @pl.when(t > 0)
        def _():
            path[...] = dot_tn(halves[t], path[...]) + dot_tn(mixed[...], dot_tn(linv[t - 1], path[...]))

        path[...] = dot_nn(linv[t], path[...])

        @pl.when((t == 4) & (core != x0))
        def _():
            swap_copy().start()

        @pl.when(t == 0)
        def _():
            for copy in loads:
                copy.wait()
            halo_wait((0, 1))
            for a in (0, 7):
                for place, col in ((1, 0), (2, 1), (3, 4), (4, 5)):
                    ext[a, place] = inner[a, col]

        for step in range(4):
            @pl.when(t == step)
            def _(step=step):
                inner_pairs(INNER[step], INNER[step + 1])

        @pl.when(t == 4)
        def _():
            out_copies[0].start()
            halo_wait(range(2, 12))
            side_pairs(0, 3)

        @pl.when((t == 4) & (core != x0))
        def _():
            swap_copy().wait()
            path[...] = swap[...]

        @pl.when(t == 5)
        def _():
            side_pairs(3, 6)
            out_copies[1].start()
            out_copies[2].start()
            products = lax.dot_general(
                coef[...], path[...], (((0,), (1,)), ((), ())), precision=highest, preferred_element_type=f32
            )
            term[...] = products.reshape(16, 48, 128)
            for d in range(1, 16):
                row_copy(d).start()
            path[...] = diag_matrix()

        @pl.when(t < LEVELS - 1)
        def _():
            cross_copy(t).wait()
            cross[...] = cross_send[t] + cross_recv[t]
            w_copy(t, (u_core, v)).wait()

        return carry

    def diag_matrix():
        down_iota = lax.broadcasted_iota(jnp.int32, (128, 128), 0)
        return jnp.where(down_iota == lax.broadcasted_iota(jnp.int32, (128, 128), 1), 1.0, 0.0).astype(f32)

    lax.fori_loop(0, LEVELS, merge, 0)
    total = term[v]
    for d in range(1, 16):
        row_copy(d).wait()
        total = total + from_row[d]
    total = dot_nt(total, path[...])
    row_sum[...] = total
    copies = []
    for d in range(1, 8):
        copy = pltpu.make_async_remote_copy(
            src_ref=row_sum, dst_ref=from_col.at[d], send_sem=col_send.at[d], recv_sem=col_recv.at[d],
            device_id=((u + d) % 8, v), device_id_type=MESH,
        )
        copy.start()
        copies.append(copy)
    root = dot_nt(mine[LEVELS, y], linv[LEVELS - 1])
    for copy in out_copies:
        copy.wait()
    for d in range(1, 8):
        copies[d - 1].wait()
        total = total + from_col[d]
    far_out[...] = dot_nt(root, total)


def solve(links, density, near_blocks, far_right, far_left, sketch, keys):
    anywhere = pl.BlockSpec(memory_space=pl.ANY)
    vmem = pl.BlockSpec(memory_space=pltpu.VMEM)
    dma = pltpu.SemaphoreType.DMA
    bf16 = jnp.bfloat16
    return pl.pallas_call(
        solver_kernel,
        out_shape=(jax.ShapeDtypeStruct((6, 6, 128, 768), bf16), jax.ShapeDtypeStruct((128, 48), f32)),
        in_specs=[pl.BlockSpec(memory_space=pltpu.SMEM)] + [anywhere] * 4 + [vmem, vmem],
        out_specs=(anywhere, vmem),
        scratch_shapes=[
            pltpu.VMEM((9, 6, 128, 768), bf16),
            pltpu.VMEM((9, 6, 128, 768), bf16),
            pltpu.VMEM((6, 6, 6, 128, 128), bf16),
            pltpu.VMEM((6, 6, 128, 128), bf16),
            pltpu.VMEM((6, 6, 128, 768), bf16),
            pltpu.VMEM((128, 768), f32),
            pltpu.VMEM((LEVELS + 1, 4, 128, 128), f32),
            pltpu.VMEM((LEVELS + 1, 4, 128, 128), f32),
            pltpu.VMEM((LEVELS + 1, 128, 128), f32),
            pltpu.VMEM((LEVELS + 1, 128, 128), f32),
            pltpu.VMEM((LEVELS, 128, 128), f32),
            pltpu.VMEM((128, 128), f32),
            pltpu.VMEM((LEVELS + 2, 128, 128), f32),
            pltpu.VMEM((LEVELS + 2, 128, 128), f32),
            pltpu.VMEM((128, 128), f32),
            pltpu.VMEM((128, 128), f32),
            pltpu.VMEM((128, 128), f32),
            pltpu.VMEM((16, 10, 8, 128), f32),
            pltpu.VMEM((LEVELS, 128, 128), f32),
            pltpu.VMEM((128, 128), f32),
            pltpu.VMEM((128, 128), f32),
            pltpu.VMEM((16, 48, 128), f32),
            pltpu.VMEM((16, 48, 128), f32),
            pltpu.VMEM((48, 128), f32),
            pltpu.VMEM((8, 48, 128), f32),
            dma((5,)), dma((3,)), dma((12,)), dma((12,)),
            dma, dma((2,)), dma((2,)),
            dma((LEVELS, 2)), dma((LEVELS, 2)), dma((LEVELS,)), dma((LEVELS,)),
            dma((LEVELS,)), dma((LEVELS,)), dma((2,)), dma((2,)), dma, dma,
            dma((16,)), dma((16,)), dma((8,)), dma((8,)),
        ],
        compiler_params=pltpu.CompilerParams(collective_id=0, has_side_effects=True, vmem_limit_bytes=60 * 2**20),
        cost_estimate=pl.CostEstimate(flops=10**10, bytes_accessed=2**25, transcendentals=0),
        name="solver",
    )(links, density, near_blocks, far_right, far_left.reshape(4, 2, 128, 128), sketch, keys)


def copy_kernel(source, target, held, in_sem, out_sem):
    reads = [pltpu.make_async_copy(source.at[i], held.at[i], in_sem.at[i]) for i in range(6)]
    writes = [pltpu.make_async_copy(held.at[i], target.at[i], out_sem.at[i]) for i in range(6)]
    for copy in reads:
        copy.start()
    for read, write in zip(reads, writes):
        read.wait()
        write.start()
    for copy in writes:
        copy.wait()


def copied(value):
    anywhere = pl.BlockSpec(memory_space=pl.ANY)
    return pl.pallas_call(
        copy_kernel,
        out_shape=jax.ShapeDtypeStruct(value.shape, value.dtype),
        in_specs=[anywhere],
        out_specs=anywhere,
        scratch_shapes=[
            pltpu.VMEM(value.shape, value.dtype), pltpu.SemaphoreType.DMA((6,)), pltpu.SemaphoreType.DMA((6,)),
        ],
        compiler_params=pltpu.CompilerParams(vmem_limit_bytes=60 * 2**20),
        name="copy_out",
    )(value)


def per_device(density, near_blocks, neighbours, far_right, far_left, sketch, patch_order):
    corrected, far_field = solve(
        neighbours, density, near_blocks, far_right, far_left, sketch, patch_order.reshape(1, 128)
    )
    return (copied(corrected), far_field)


def solution(mesh):
    in_specs = (
        P("pu", "pv", None, None),
        P("pu", "pv", None, None, None),
        P("pu", "pv", None),
        P("pu", "pv", None, None),
        P("pu", "pv", None, None),
        P(),
        P(),
    )
    out_specs = (P("pu", "pv", None, None), P("pu", "pv"))
    return jax.shard_map(
        per_device, mesh=mesh, in_specs=in_specs, out_specs=out_specs, check_vma=False
    )
```

```python
import functools

import jax
import jax.numpy as jnp
from jax import lax
from jax.experimental import pallas as pl
from jax.experimental.pallas import tpu as pltpu
from jax.sharding import PartitionSpec as P

MESH = pl.DeviceIdType.MESH
highest = lax.Precision.HIGHEST
f32 = jnp.float32
LEVELS = 7
INNER = (0, 3, 6, 9, 12)


def dot_nn(a, b):
    return lax.dot_general(a, b, (((1,), (0,)), ((), ())), precision=highest, preferred_element_type=f32)


def dot_tn(a, b):
    return lax.dot_general(a, b, (((0,), (0,)), ((), ())), precision=highest, preferred_element_type=f32)


def dot_nt(a, b):
    return lax.dot_general(a, b, (((1,), (1,)), ((), ())), precision=highest, preferred_element_type=f32)


def tile(x):
    return jnp.broadcast_to(x, (8, 128))


def tree_sum(terms):
    while len(terms) > 1:
        terms = [terms[i] + terms[i + 1] if i + 1 < len(terms) else terms[i] for i in range(0, len(terms), 2)]
    return terms[0]


def cholesky_inverse(gram, out_ref, panels):
    groups = 16
    row = lax.broadcasted_iota(jnp.int32, (8, 128), 0)
    lane = lax.broadcasted_iota(jnp.int32, (8, 128), 1)
    left = [gram[8 * g : 8 * g + 8, :] for g in range(groups)]
    right = [jnp.where(lane == row + 8 * g, 1.0, 0.0).astype(f32) for g in range(groups)]
    for b in range(groups):
        base = 8 * b
        last = b == groups - 1
        cols = [[tile(left[g][:, base + k : base + k + 1]) for k in range(8)] for g in range(b, groups)]
        for k in range(8):
            panels[b, k] = cols[0][k]
        panels[b, 8] = left[b]
        panels[b, 9] = right[b]
        d = [[tile(panels[b, k, i : i + 1, :]) for k in range(i + 1)] for i in range(8)]
        low = [[None] * 8 for _ in range(8)]
        inv = [[None] * 8 for _ in range(8)]
        for k in range(0, 8, 2):
            p, q, r = d[k][k], d[k + 1][k], d[k + 1][k + 1]
            scale = lax.rsqrt(p)
            second = lax.rsqrt(p * r - q * q)
            both = scale * second
            low[k + 1][k] = q * scale
            for i in range(k + 2, 8):
                low[i][k] = d[i][k] * scale
                low[i][k + 1] = (p * d[i][k + 1] - d[i][k] * q) * both
            for m in range(k + 2, 8):
                for i in range(m, 8):
                    d[i][m] = d[i][m] - (low[i][k] * low[m][k] + low[i][k + 1] * low[m][k + 1])
            for n, pivot in ((k, scale), (k + 1, p * both)):
                inv[n][n] = pivot
                for j in range(n):
                    inv[n][j] = -(pivot * tree_sum([low[n][h] * inv[h][j] for h in range(j, n)]))

        def solved(panel):
            return [tree_sum([inv[i][k] * panel[k] for k in range(i + 1)]) for i in range(8)]

        def solved_again(up):
            return [tree_sum([inv[i][k] * up[i] for i in range(k, 8)]) for k in range(8)]

        up_right = solved([tile(panels[b, 9, k : k + 1, :]) for k in range(8)])
        for i in range(8):
            out_ref[base + i : base + i + 1, :] = up_right[i][0:1, :]
        if last:
            break
        full_left = solved_again(solved([tile(panels[b, 8, k : k + 1, :]) for k in range(8)]))
        full_right = solved_again(up_right)
        for g in range(b + 1, groups):
            c = cols[g - b]
            left[g] = left[g] - tree_sum([c[k] * full_left[k] for k in range(8)])
            right[g] = right[g] - tree_sum([c[k] * full_right[k] for k in range(8)])


def flip(index, bit):
    return index + bit - 2 * bit * ((index // bit) % 2)


def near_pair(i, cols, places, links, source, near, right, out, coef):
    done = []
    for j, place in zip(cols, places):
        where = []
        for s in range(6):
            e = links[i, j, s]
            down = (e * 11) // 32
            across = e - 3 * down
            where.append((jnp.where(e < 9, i + down, 8), jnp.where(e < 9, place + across - 1, 0)))
        lhs = jnp.concatenate([near[i, j, s] for s in range(6)], axis=1)
        rhs = jnp.concatenate([source[a, b] for a, b in where], axis=0)
        summed = jnp.dot(lhs, rhs, preferred_element_type=f32)
        block = (source[i + 1, place].astype(f32) + summed).astype(jnp.bfloat16)
        out[i, j] = block
        done.append(block)
    lhs = jnp.concatenate([right[i, j] for j in cols], axis=0)
    coef[...] += lax.dot_general(
        lhs, jnp.concatenate(done, axis=0), (((0,), (0,)), ((), ())), preferred_element_type=f32
    )


def split(value):
    high = value.astype(jnp.bfloat16)
    return high, (value - high.astype(f32)).astype(jnp.bfloat16)


def dot_sum(a, b, wide):
    a_high, a_low = split(a)
    b_high, b_low = split(b)
    return jnp.dot(
        jnp.concatenate([a_high, b_high, a_high, b_high, a_low, b_low], axis=1), wide, preferred_element_type=f32
    )


def widened(a, b):
    a_high, a_low = split(a)
    b_high, b_low = split(b)
    return jnp.concatenate([a_high, b_high, a_low, b_low, a_high, b_high], axis=0)


def solver_kernel(
    links, density, near_hbm, right_hbm, leaf, sketch, keys, corrected, far_out,
    ext, inner, near, right, out, coef,
    mine, other, w_mine, w_other, halves, base, cross_send, cross_recv, cross, gram, mixed, panels, linv, path, swap,
    term, from_row, row_sum, from_col,
    load_sem, out_sem, halo_send, halo_recv,
    leaf_local, leaf_send, leaf_recv, y_send, y_recv, w_send, w_recv, c_send, c_recv, g_send, g_recv, s_send, s_recv,
    row_send, row_recv, col_send, col_recv,
):
    u = lax.axis_index("pu")
    v = lax.axis_index("pv")
    core = u % 2
    y = u // 2
    x0 = v % 2
    u_core = flip(u, 1)
    v_next = flip(v, 1)
    partners = {1: (u, flip(v, 2)), 2: (u, flip(v, 4)), 3: (u, flip(v, 8)), 4: (u, v_next), 5: (flip(u, 2), v), 6: (flip(u, 4), v)}
    barrier = pltpu.get_barrier_semaphore()
    peers = list(partners.values()) + [(u_core, v), (u_core, v_next)]
    for du in (7, 0, 1):
        for dv in (15, 0, 1):
            if du or dv:
                peers.append(((u + du) % 8, (v + dv) % 16))
    for peer in peers:
        pl.semaphore_signal(barrier, inc=1, device_id=peer, device_id_type=MESH)
    loads = [
        pltpu.make_async_copy(near_hbm, near, load_sem.at[0]),
        pltpu.make_async_copy(density, inner.at[1:7], load_sem.at[1]),
        pltpu.make_async_copy(right_hbm, right, load_sem.at[2]),
        pltpu.make_async_copy(density.at[:, 0:2], ext.at[1:7, 1:3], load_sem.at[3]),
        pltpu.make_async_copy(density.at[:, 4:6], ext.at[1:7, 3:5], load_sem.at[4]),
    ]
    for copy in loads:
        copy.start()
    key = keys[...]
    patch = lax.broadcasted_iota(jnp.int32, (1, 128), 1)
    rows = patch // 16
    cols = patch % 16
    host_row = 2 * y + x0

    def least(mask):
        return jnp.min(jnp.where(mask, key, 1 << 20), axis=1, keepdims=True)

    here = rows == host_row
    even = v - x0
    pairs = [(here & (cols == even), here & (cols == even + 1))]
    for bit in (2, 4, 8):
        pairs.append((here & (cols // bit == v // bit), here & (cols // bit == flip(v, bit) // bit)))
    pairs.append((here, rows == 2 * y + 1 - x0))
    for bit in (2, 4):
        pairs.append((rows // bit == u // bit, rows // bit == flip(u, bit) // bit))
    first = sketch[0:128, :]
    second = sketch[128:256, :]
    for t, (own, sibling) in enumerate(pairs):
        leads = jnp.broadcast_to((least(own) < least(sibling)).astype(f32), (128, 128)) > 0.5
        halves[t] = jnp.where(leads, first, second)
        if t == 0:
            w_mine[0] = halves[0]
            w_other[0] = jnp.where(leads, second, first)
    base[...] = dot_tn(sketch[...], sketch[...])
    pl.semaphore_wait(barrier, len(peers))

    def leaf_copy(part, slot_ref, to, slot):
        return pltpu.make_async_remote_copy(
            src_ref=leaf.at[:, part], dst_ref=slot_ref.at[0], send_sem=leaf_send.at[part],
            recv_sem=leaf_recv.at[slot], device_id=to, device_id_type=MESH,
        )

    slots = (mine, other)
    for c in range(2):
        for x in range(2):
            @pl.when((core == c) & (x0 == x))
            def _(c=c, x=x):
                if c == x:
                    leaf_copy(1 - c, slots[x], (u_core, v), x).start()
                    pltpu.make_async_copy(leaf.at[:, c], slots[x].at[0], leaf_local).start()
                else:
                    leaf_copy(c, slots[x], (u, v_next), x).start()
                    leaf_copy(1 - c, slots[x], (u_core, v_next), x).start()
    up, down, west, east = u > 0, u < 7, v > 0, v < 15
    turn_west, turn_east = v % 4 == 0, v % 4 == 3
    halo = [
        (density.at[0], inner.at[7], (u - 1, v), up, down, None),
        (density.at[5], inner.at[0], (u + 1, v), down, up, None),
    ]
    for r in range(3):
        span = slice(2 * r, 2 * r + 2)
        to_span = slice(2 * r + 1, 2 * r + 3)
        halo.append((density.at[span, 0], ext.at[to_span, 5], (u, v - 1), west, east, turn_west))
        halo.append((density.at[span, 5], ext.at[to_span, 0], (u, v + 1), east, west, turn_east))
    halo += [
        (density.at[0, 0], ext.at[7, 5], (u - 1, v - 1), up & west, down & east, turn_west),
        (density.at[5, 5], ext.at[0, 0], (u + 1, v + 1), down & east, up & west, turn_east),
        (density.at[0, 5], ext.at[7, 0], (u - 1, v + 1), up & east, down & west, turn_east),
        (density.at[5, 0], ext.at[0, 5], (u + 1, v - 1), down & west, up & east, turn_west),
    ]

    def halo_copy(n):
        source, target, to = halo[n][:3]
        return pltpu.make_async_remote_copy(
            src_ref=source, dst_ref=target, send_sem=halo_send.at[n], recv_sem=halo_recv.at[n],
            device_id=to, device_id_type=MESH,
        )

    def halo_start(numbers, only=None):
        for n in numbers:
            due = halo[n][3]
            if only is not None:
                due = due & only

            @pl.when(due)
            def _(n=n):
                halo_copy(n).start()

    def halo_wait(numbers):
        for n in numbers:
            @pl.when(halo[n][3])
            def _(n=n):
                halo_copy(n).wait_send()

            @pl.when(halo[n][4])
            def _(n=n):
                halo_copy(n).wait_recv()

    even_v, odd_v = x0 == 0, x0 == 1
    halo_start((0, 1))
    halo_start((2,), even_v)
    halo_start((3,), odd_v)
    halo_start((4,), turn_west)
    halo_start((5,), turn_east)
    zero = jnp.zeros((128, 768), jnp.bfloat16)
    ext[8, 0] = zero
    inner[8, 0] = zero
    for edge, target, cells in (
        (u == 0, inner, [(0, n) for n in range(6)]),
        (u == 7, inner, [(7, n) for n in range(6)]),
        (u == 0, ext, [(0, 0), (0, 5)]),
        (u == 7, ext, [(7, 0), (7, 5)]),
        (v == 0, ext, [(n, 0) for n in range(8)]),
        (v == 15, ext, [(n, 5) for n in range(8)]),
    ):
        @pl.when(edge)
        def _(target=target, cells=cells):
            for a, b in cells:
                target[a, b] = zero
    coef[...] = jnp.zeros_like(coef)

    def inner_pairs(low, high):
        def step(n, carry):
            j = 1 + 2 * (n % 2)
            near_pair(n // 2, (j, j + 1), (j, j + 1), links, inner, near, right, out, coef)
            return carry

        lax.fori_loop(low, high, step, 0)

    def side_pairs(low, high):
        def step(i, carry):
            near_pair(i, (0, 5), (1, 4), links, ext, near, right, out, coef)
            return carry

        lax.fori_loop(low, high, step, 0)

    for c in range(2):
        for x in range(2):
            @pl.when((core == c) & (x0 == x))
            def _(c=c, x=x):
                if c == x:
                    pltpu.make_async_copy(leaf.at[:, c], slots[x].at[0], leaf_local).wait()
                    leaf_copy(1 - c, slots[x], (u_core, v), x).wait_send()
                    leaf_copy(0, slots[1 - x], (u_core, v), 1 - x).wait_recv()
                else:
                    for part in range(2):
                        leaf_copy(part, slots[x], (u_core, v), x).wait_send()
                    for slot in range(2):
                        leaf_copy(0, slots[slot], (u_core, v), slot).wait_recv()

    halo_start((2,), odd_v)
    halo_start((3,), even_v)
    straight_west, straight_east = jnp.logical_not(turn_west), jnp.logical_not(turn_east)

    def y_copy(t, part, to):
        span = slice(2 * part, 2 * part + 2)
        return pltpu.make_async_remote_copy(
            src_ref=mine.at[t + 1, span], dst_ref=other.at[t + 1, span],
            send_sem=y_send.at[t, part], recv_sem=y_recv.at[t, part],
            device_id=to, device_id_type=MESH,
        )

    def w_copy(t, to):
        return pltpu.make_async_remote_copy(
            src_ref=w_mine.at[t + 1], dst_ref=w_other.at[t + 1], send_sem=w_send.at[t], recv_sem=w_recv.at[t],
            device_id=to, device_id_type=MESH,
        )

    def cross_copy(t):
        return pltpu.make_async_remote_copy(
            src_ref=cross_send.at[t], dst_ref=cross_recv.at[t], send_sem=c_send.at[t], recv_sem=c_recv.at[t],
            device_id=(u_core, v), device_id_type=MESH,
        )

    def leaf_gram_copy(kind):
        return pltpu.make_async_remote_copy(
            src_ref=cross_send.at[LEVELS + kind], dst_ref=cross_recv.at[LEVELS + kind], send_sem=g_send.at[kind],
            recv_sem=g_recv.at[kind], device_id=(u_core, v), device_id_type=MESH,
        )

    def swap_copy():
        return pltpu.make_async_remote_copy(
            src_ref=path, dst_ref=swap, send_sem=s_send, recv_sem=s_recv,
            device_id=(u_core, v_next), device_id_type=MESH,
        )

    def row_copy(d):
        to = (v + d) % 16
        return pltpu.make_async_remote_copy(
            src_ref=term.at[to], dst_ref=from_row.at[d], send_sem=row_send.at[d], recv_sem=row_recv.at[d],
            device_id=(u, to), device_id_type=MESH,
        )

    out_copies = [
        pltpu.make_async_copy(out.at[:, 1:5], corrected.at[:, 1:5], out_sem.at[0]),
        pltpu.make_async_copy(out.at[:, 0], corrected.at[:, 0], out_sem.at[1]),
        pltpu.make_async_copy(out.at[:, 5], corrected.at[:, 5], out_sem.at[2]),
    ]

    def merge(t, carry):
        wide = widened(w_mine[t], w_other[t])
        for part in range(2):
            span = slice(2 * part, 2 * part + 2)
            both = dot_sum(mine[t, span].reshape(256, 128), other[t, span].reshape(256, 128), wide)
            mine[t + 1, span] = both.reshape(2, 128, 128)
            for step in range(LEVELS - 1):
                @pl.when(t == step)
                def _(step=step, part=part):
                    y_copy(step, part, partners[step + 1]).start()

        @pl.when(t == 1)
        def _():
            halo_start((4, 8), straight_west)
            halo_start((5, 9), straight_east)

        @pl.when(t == 2)
        def _():
            halo_start((6, 11), straight_west)
            halo_start((7, 10), straight_east)

        @pl.when(t == 3)
        def _():
            halo_start((6, 8, 11), turn_west)
            halo_start((7, 9, 10), turn_east)

        @pl.when(t == 0)
        def _():
            merged = mine[1].reshape(512, 128)
            part = dot_tn(merged, merged)
            cross_send[LEVELS] = part
            leaf_gram_copy(0).start()
            ours = dot_tn(merged, mine[0].reshape(512, 128))
            theirs = dot_tn(merged, other[0].reshape(512, 128))
            cross_send[LEVELS + 1] = jnp.where(core == 0, theirs, ours)
            leaf_gram_copy(1).start()
            leaf_gram_copy(0).wait()
            gram[...] = part + cross_recv[LEVELS]
            leaf_gram_copy(1).wait()
            path[...] = jnp.where(core == 0, ours, theirs) + cross_recv[LEVELS + 1]

        @pl.when(t > 0)
        def _():
            mixed[...] = dot_nn(cross[...], w_other[t])
            half = dot_tn(w_mine[t], mixed[...])
            gram[...] = base[...] + half + half.T

        cholesky_inverse(gram, linv.at[t], panels)

        @pl.when(t < LEVELS - 1)
        def _():
            w_mine[t + 1] = dot_tn(linv[t], halves[t + 1])

        for step in range(LEVELS - 1):
            @pl.when(t == step)
            def _(step=step):
                w_copy(step, partners[step + 1]).start()

        @pl.when(t > 0)
        def _():
            path[...] = dot_tn(halves[t], path[...]) + dot_tn(mixed[...], dot_tn(linv[t - 1], path[...]))

        path[...] = dot_nn(linv[t], path[...])

        @pl.when(t < LEVELS - 1)
        def _():
            y_copy(t, 0, (u_core, v)).wait()
            part = dot_tn(mine[t + 1, 0:2].reshape(256, 128), other[t + 1, 0:2].reshape(256, 128))
            y_copy(t, 1, (u_core, v)).wait()
            part = part + dot_tn(mine[t + 1, 2:4].reshape(256, 128), other[t + 1, 2:4].reshape(256, 128))
            cross_send[t] = part
            cross_copy(t).start()

        @pl.when((t == 4) & (core != x0))
        def _():
            swap_copy().start()

        @pl.when(t == 0)
        def _():
            for copy in loads:
                copy.wait()
            halo_wait((0, 1))
            for a in (0, 7):
                for place, col in ((1, 0), (2, 1), (3, 4), (4, 5)):
                    ext[a, place] = inner[a, col]

        for step in range(4):
            @pl.when(t == step)
            def _(step=step):
                inner_pairs(INNER[step], INNER[step + 1])

        @pl.when(t == 4)
        def _():
            out_copies[0].start()
            halo_wait(range(2, 12))
            side_pairs(0, 3)

        @pl.when((t == 4) & (core != x0))
        def _():
            swap_copy().wait()
            path[...] = swap[...]

        @pl.when(t == 5)
        def _():
            side_pairs(3, 6)
            out_copies[1].start()
            out_copies[2].start()
            products = lax.dot_general(
                coef[...], path[...], (((0,), (1,)), ((), ())), precision=highest, preferred_element_type=f32
            )
            term[...] = products.reshape(16, 48, 128)
            for d in range(1, 16):
                row_copy(d).start()
            path[...] = diag_matrix()

        @pl.when(t < LEVELS - 1)
        def _():
            cross_copy(t).wait()
            cross[...] = cross_send[t] + cross_recv[t]
            w_copy(t, (u_core, v)).wait()

        return carry

    def diag_matrix():
        down_iota = lax.broadcasted_iota(jnp.int32, (128, 128), 0)
        return jnp.where(down_iota == lax.broadcasted_iota(jnp.int32, (128, 128), 1), 1.0, 0.0).astype(f32)

    lax.fori_loop(0, LEVELS, merge, 0)
    total = term[v]
    for d in range(1, 16):
        row_copy(d).wait()
        total = total + from_row[d]
    total = dot_nt(total, path[...])
    row_sum[...] = total
    copies = []
    for d in range(1, 8):
        copy = pltpu.make_async_remote_copy(
            src_ref=row_sum, dst_ref=from_col.at[d], send_sem=col_send.at[d], recv_sem=col_recv.at[d],
            device_id=((u + d) % 8, v), device_id_type=MESH,
        )
        copy.start()
        copies.append(copy)
    root = dot_nt(mine[LEVELS, y], linv[LEVELS - 1])
    for copy in out_copies:
        copy.wait()
    for d in range(1, 8):
        copies[d - 1].wait()
        total = total + from_col[d]
    far_out[...] = dot_nt(root, total)


def solve(links, density, near_blocks, far_right, far_left, sketch, keys):
    anywhere = pl.BlockSpec(memory_space=pl.ANY)
    vmem = pl.BlockSpec(memory_space=pltpu.VMEM)
    dma = pltpu.SemaphoreType.DMA
    bf16 = jnp.bfloat16
    return pl.pallas_call(
        solver_kernel,
        out_shape=(jax.ShapeDtypeStruct((6, 6, 128, 768), bf16), jax.ShapeDtypeStruct((128, 48), f32)),
        in_specs=[pl.BlockSpec(memory_space=pltpu.SMEM)] + [anywhere] * 4 + [vmem, vmem],
        out_specs=(anywhere, vmem),
        scratch_shapes=[
            pltpu.VMEM((9, 6, 128, 768), bf16),
            pltpu.VMEM((9, 6, 128, 768), bf16),
            pltpu.VMEM((6, 6, 6, 128, 128), bf16),
            pltpu.VMEM((6, 6, 128, 128), bf16),
            pltpu.VMEM((6, 6, 128, 768), bf16),
            pltpu.VMEM((128, 768), f32),
            pltpu.VMEM((LEVELS + 1, 4, 128, 128), f32),
            pltpu.VMEM((LEVELS + 1, 4, 128, 128), f32),
            pltpu.VMEM((LEVELS + 1, 128, 128), f32),
            pltpu.VMEM((LEVELS + 1, 128, 128), f32),
            pltpu.VMEM((LEVELS, 128, 128), f32),
            pltpu.VMEM((128, 128), f32),
            pltpu.VMEM((LEVELS + 2, 128, 128), f32),
            pltpu.VMEM((LEVELS + 2, 128, 128), f32),
            pltpu.VMEM((128, 128), f32),
            pltpu.VMEM((128, 128), f32),
            pltpu.VMEM((128, 128), f32),
            pltpu.VMEM((16, 10, 8, 128), f32),
            pltpu.VMEM((LEVELS, 128, 128), f32),
            pltpu.VMEM((128, 128), f32),
            pltpu.VMEM((128, 128), f32),
            pltpu.VMEM((16, 48, 128), f32),
            pltpu.VMEM((16, 48, 128), f32),
            pltpu.VMEM((48, 128), f32),
            pltpu.VMEM((8, 48, 128), f32),
            dma((5,)), dma((3,)), dma((12,)), dma((12,)),
            dma, dma((2,)), dma((2,)),
            dma((LEVELS, 2)), dma((LEVELS, 2)), dma((LEVELS,)), dma((LEVELS,)),
            dma((LEVELS,)), dma((LEVELS,)), dma((2,)), dma((2,)), dma, dma,
            dma((16,)), dma((16,)), dma((8,)), dma((8,)),
        ],
        compiler_params=pltpu.CompilerParams(collective_id=0, has_side_effects=True, vmem_limit_bytes=60 * 2**20),
        cost_estimate=pl.CostEstimate(flops=10**10, bytes_accessed=2**25, transcendentals=0),
        name="solver",
    )(links, density, near_blocks, far_right, far_left.reshape(4, 2, 128, 128), sketch, keys)


def copy_kernel(source, target, held, in_sem, out_sem):
    reads = [pltpu.make_async_copy(source.at[i], held.at[i], in_sem.at[i]) for i in range(6)]
    writes = [pltpu.make_async_copy(held.at[i], target.at[i], out_sem.at[i]) for i in range(6)]
    for copy in reads:
        copy.start()
    for read, write in zip(reads, writes):
        read.wait()
        write.start()
    for copy in writes:
        copy.wait()


def copied(value):
    anywhere = pl.BlockSpec(memory_space=pl.ANY)
    return pl.pallas_call(
        copy_kernel,
        out_shape=jax.ShapeDtypeStruct(value.shape, value.dtype),
        in_specs=[anywhere],
        out_specs=anywhere,
        scratch_shapes=[
            pltpu.VMEM(value.shape, value.dtype), pltpu.SemaphoreType.DMA((6,)), pltpu.SemaphoreType.DMA((6,)),
        ],
        compiler_params=pltpu.CompilerParams(vmem_limit_bytes=60 * 2**20),
        name="copy_out",
    )(value)


def per_device(density, near_blocks, neighbours, far_right, far_left, sketch, patch_order):
    corrected, far_field = solve(
        neighbours, density, near_blocks, far_right, far_left, sketch, patch_order.reshape(1, 128)
    )
    return (copied(corrected), far_field)


def solution(mesh):
    in_specs = (
        P("pu", "pv", None, None),
        P("pu", "pv", None, None, None),
        P("pu", "pv", None),
        P("pu", "pv", None, None),
        P("pu", "pv", None, None),
        P(),
        P(),
    )
    out_specs = (P("pu", "pv", None, None), P("pu", "pv"))
    return jax.shard_map(
        per_device, mesh=mesh, in_specs=in_specs, out_specs=out_specs, check_vma=False
    )
```

```python
import functools

import jax
import jax.numpy as jnp
from jax import lax
from jax.experimental import pallas as pl
from jax.experimental.pallas import tpu as pltpu
from jax.sharding import PartitionSpec as P

MESH = pl.DeviceIdType.MESH
highest = lax.Precision.HIGHEST
f32 = jnp.float32
LEVELS = 7
INNER = (0, 3, 6, 9, 12)


def dot_nn(a, b):
    return lax.dot_general(a, b, (((1,), (0,)), ((), ())), precision=highest, preferred_element_type=f32)


def dot_tn(a, b):
    return lax.dot_general(a, b, (((0,), (0,)), ((), ())), precision=highest, preferred_element_type=f32)


def dot_nt(a, b):
    return lax.dot_general(a, b, (((1,), (1,)), ((), ())), precision=highest, preferred_element_type=f32)


def tile(x):
    return jnp.broadcast_to(x, (8, 128))


def tree_sum(terms):
    while len(terms) > 1:
        terms = [terms[i] + terms[i + 1] if i + 1 < len(terms) else terms[i] for i in range(0, len(terms), 2)]
    return terms[0]


def cholesky_inverse(gram, out_ref, panels):
    groups = 16
    row = lax.broadcasted_iota(jnp.int32, (8, 128), 0)
    lane = lax.broadcasted_iota(jnp.int32, (8, 128), 1)
    left = [gram[8 * g : 8 * g + 8, :] for g in range(groups)]
    right = [jnp.where(lane == row + 8 * g, 1.0, 0.0).astype(f32) for g in range(groups)]
    for b in range(groups):
        base = 8 * b
        last = b == groups - 1
        cols = [[tile(left[g][:, base + k : base + k + 1]) for k in range(8)] for g in range(b, groups)]
        for k in range(8):
            panels[b, k] = cols[0][k]
        panels[b, 8] = left[b]
        panels[b, 9] = right[b]
        d = [[tile(panels[b, k, i : i + 1, :]) for k in range(i + 1)] for i in range(8)]
        low = [[None] * 8 for _ in range(8)]
        inv = [[None] * 8 for _ in range(8)]
        for k in range(0, 8, 2):
            p, q, r = d[k][k], d[k + 1][k], d[k + 1][k + 1]
            scale = lax.rsqrt(p)
            second = lax.rsqrt(p * r - q * q)
            both = scale * second
            low[k + 1][k] = q * scale
            for i in range(k + 2, 8):
                low[i][k] = d[i][k] * scale
                low[i][k + 1] = (p * d[i][k + 1] - d[i][k] * q) * both
            for m in range(k + 2, 8):
                for i in range(m, 8):
                    d[i][m] = d[i][m] - (low[i][k] * low[m][k] + low[i][k + 1] * low[m][k + 1])
            for n, pivot in ((k, scale), (k + 1, p * both)):
                inv[n][n] = pivot
                for j in range(n):
                    inv[n][j] = -(pivot * tree_sum([low[n][h] * inv[h][j] for h in range(j, n)]))

        def solved(panel):
            return [tree_sum([inv[i][k] * panel[k] for k in range(i + 1)]) for i in range(8)]

        def solved_again(up):
            return [tree_sum([inv[i][k] * up[i] for i in range(k, 8)]) for k in range(8)]

        up_right = solved([tile(panels[b, 9, k : k + 1, :]) for k in range(8)])
        for i in range(8):
            out_ref[base + i : base + i + 1, :] = up_right[i][0:1, :]
        if last:
            break
        full_left = solved_again(solved([tile(panels[b, 8, k : k + 1, :]) for k in range(8)]))
        full_right = solved_again(up_right)
        for g in range(b + 1, groups):
            c = cols[g - b]
            left[g] = left[g] - tree_sum([c[k] * full_left[k] for k in range(8)])
            right[g] = right[g] - tree_sum([c[k] * full_right[k] for k in range(8)])


def flip(index, bit):
    return index + bit - 2 * bit * ((index // bit) % 2)


def near_pair(i, cols, places, links, source, near, right, out, coef):
    done = []
    for j, place in zip(cols, places):
        where = []
        for s in range(6):
            e = links[i, j, s]
            down = (e * 11) // 32
            across = e - 3 * down
            where.append((jnp.where(e < 9, i + down, 8), jnp.where(e < 9, place + across - 1, 0)))
        lhs = jnp.concatenate([near[i, j, s] for s in range(6)], axis=1)
        rhs = jnp.concatenate([source[a, b] for a, b in where], axis=0)
        summed = jnp.dot(lhs, rhs, preferred_element_type=f32)
        block = (source[i + 1, place].astype(f32) + summed).astype(jnp.bfloat16)
        out[i, j] = block
        done.append(block)
    lhs = jnp.concatenate([right[i, j] for j in cols], axis=0)
    coef[...] += lax.dot_general(
        lhs, jnp.concatenate(done, axis=0), (((0,), (0,)), ((), ())), preferred_element_type=f32
    )


def split(value):
    high = value.astype(jnp.bfloat16)
    return high, (value - high.astype(f32)).astype(jnp.bfloat16)


def dot_sum(a, b, wide):
    a_high, a_low = split(a)
    b_high, b_low = split(b)
    return jnp.dot(
        jnp.concatenate([a_high, b_high, a_high, b_high, a_low, b_low], axis=1), wide, preferred_element_type=f32
    )


def widened(a, b):
    a_high, a_low = split(a)
    b_high, b_low = split(b)
    return jnp.concatenate([a_high, b_high, a_low, b_low, a_high, b_high], axis=0)


def solver_kernel(
    links, density, near_hbm, right_hbm, leaf, sketch, keys, corrected, far_out,
    ext, inner, near, right, out, coef,
    mine, other, w_mine, w_other, halves, base, cross_send, cross_recv, cross, gram, mixed, panels, linv, path, swap,
    term, from_row, row_sum, from_col,
    load_sem, out_sem, halo_send, halo_recv,
    leaf_local, leaf_send, leaf_recv, y_send, y_recv, w_send, w_recv, c_send, c_recv, g_send, g_recv, s_send, s_recv,
    row_send, row_recv, col_send, col_recv,
):
    u = lax.axis_index("pu")
    v = lax.axis_index("pv")
    core = u % 2
    y = u // 2
    x0 = v % 2
    u_core = flip(u, 1)
    v_next = flip(v, 1)
    partners = {1: (u, flip(v, 2)), 2: (u, flip(v, 4)), 3: (u, flip(v, 8)), 4: (u, v_next), 5: (flip(u, 2), v), 6: (flip(u, 4), v)}
    barrier = pltpu.get_barrier_semaphore()
    peers = list(partners.values()) + [(u_core, v), (u_core, v_next)]
    for du in (7, 0, 1):
        for dv in (15, 0, 1):
            if du or dv:
                peers.append(((u + du) % 8, (v + dv) % 16))
    for peer in peers:
        pl.semaphore_signal(barrier, inc=1, device_id=peer, device_id_type=MESH)
    loads = [
        pltpu.make_async_copy(near_hbm, near, load_sem.at[0]),
        pltpu.make_async_copy(density, inner.at[1:7], load_sem.at[1]),
        pltpu.make_async_copy(right_hbm, right, load_sem.at[2]),
        pltpu.make_async_copy(density.at[:, 0:2], ext.at[1:7, 1:3], load_sem.at[3]),
        pltpu.make_async_copy(density.at[:, 4:6], ext.at[1:7, 3:5], load_sem.at[4]),
    ]
    for copy in loads:
        copy.start()
    key = keys[...]
    patch = lax.broadcasted_iota(jnp.int32, (1, 128), 1)
    rows = patch // 16
    cols = patch % 16
    host_row = 2 * y + x0

    def least(mask):
        return jnp.min(jnp.where(mask, key, 1 << 20), axis=1, keepdims=True)

    here = rows == host_row
    even = v - x0
    pairs = [(here & (cols == even), here & (cols == even + 1))]
    for bit in (2, 4, 8):
        pairs.append((here & (cols // bit == v // bit), here & (cols // bit == flip(v, bit) // bit)))
    pairs.append((here, rows == 2 * y + 1 - x0))
    for bit in (2, 4):
        pairs.append((rows // bit == u // bit, rows // bit == flip(u, bit) // bit))
    first = sketch[0:128, :]
    second = sketch[128:256, :]
    for t, (own, sibling) in enumerate(pairs):
        leads = jnp.broadcast_to((least(own) < least(sibling)).astype(f32), (128, 128)) > 0.5
        halves[t] = jnp.where(leads, first, second)
        if t == 0:
            w_mine[0] = halves[0]
            w_other[0] = jnp.where(leads, second, first)
    base[...] = dot_tn(sketch[...], sketch[...])
    pl.semaphore_wait(barrier, len(peers))

    def leaf_copy(part, slot_ref, to, slot):
        return pltpu.make_async_remote_copy(
            src_ref=leaf.at[:, part], dst_ref=slot_ref.at[0], send_sem=leaf_send.at[part],
            recv_sem=leaf_recv.at[slot], device_id=to, device_id_type=MESH,
        )

    slots = (mine, other)
    for c in range(2):
        for x in range(2):
            @pl.when((core == c) & (x0 == x))
            def _(c=c, x=x):
                if c == x:
                    leaf_copy(1 - c, slots[x], (u_core, v), x).start()
                    pltpu.make_async_copy(leaf.at[:, c], slots[x].at[0], leaf_local).start()
                else:
                    leaf_copy(c, slots[x], (u, v_next), x).start()
                    leaf_copy(1 - c, slots[x], (u_core, v_next), x).start()
    up, down, west, east = u > 0, u < 7, v > 0, v < 15
    turn_west, turn_east = v % 4 == 0, v % 4 == 3
    halo = [
        (density.at[0], inner.at[7], (u - 1, v), up, down, None),
        (density.at[5], inner.at[0], (u + 1, v), down, up, None),
    ]
    for r in range(3):
        span = slice(2 * r, 2 * r + 2)
        to_span = slice(2 * r + 1, 2 * r + 3)
        halo.append((density.at[span, 0], ext.at[to_span, 5], (u, v - 1), west, east, turn_west))
        halo.append((density.at[span, 5], ext.at[to_span, 0], (u, v + 1), east, west, turn_east))
    halo += [
        (density.at[0, 0], ext.at[7, 5], (u - 1, v - 1), up & west, down & east, turn_west),
        (density.at[5, 5], ext.at[0, 0], (u + 1, v + 1), down & east, up & west, turn_east),
        (density.at[0, 5], ext.at[7, 0], (u - 1, v + 1), up & east, down & west, turn_east),
        (density.at[5, 0], ext.at[0, 5], (u + 1, v - 1), down & west, up & east, turn_west),
    ]

    def halo_copy(n):
        source, target, to = halo[n][:3]
        return pltpu.make_async_remote_copy(
            src_ref=source, dst_ref=target, send_sem=halo_send.at[n], recv_sem=halo_recv.at[n],
            device_id=to, device_id_type=MESH,
        )

    def halo_start(numbers, only=None):
        for n in numbers:
            due = halo[n][3]
            if only is not None:
                due = due & only

            @pl.when(due)
            def _(n=n):
                halo_copy(n).start()

    def halo_wait(numbers):
        for n in numbers:
            @pl.when(halo[n][3])
            def _(n=n):
                halo_copy(n).wait_send()

            @pl.when(halo[n][4])
            def _(n=n):
                halo_copy(n).wait_recv()

    even_v, odd_v = x0 == 0, x0 == 1
    halo_start((0, 1))
    halo_start((2,), even_v)
    halo_start((3,), odd_v)
    halo_start((4,), turn_west)
    halo_start((5,), turn_east)
    zero = jnp.zeros((128, 768), jnp.bfloat16)
    ext[8, 0] = zero
    inner[8, 0] = zero
    for edge, target, cells in (
        (u == 0, inner, [(0, n) for n in range(6)]),
        (u == 7, inner, [(7, n) for n in range(6)]),
        (u == 0, ext, [(0, 0), (0, 5)]),
        (u == 7, ext, [(7, 0), (7, 5)]),
        (v == 0, ext, [(n, 0) for n in range(8)]),
        (v == 15, ext, [(n, 5) for n in range(8)]),
    ):
        @pl.when(edge)
        def _(target=target, cells=cells):
            for a, b in cells:
                target[a, b] = zero
    coef[...] = jnp.zeros_like(coef)

    def inner_pairs(low, high):
        def step(n, carry):
            j = 1 + 2 * (n % 2)
            near_pair(n // 2, (j, j + 1), (j, j + 1), links, inner, near, right, out, coef)
            return carry

        lax.fori_loop(low, high, step, 0)

    def side_pairs(low, high):
        def step(i, carry):
            near_pair(i, (0, 5), (1, 4), links, ext, near, right, out, coef)
            return carry

        lax.fori_loop(low, high, step, 0)

    for c in range(2):
        for x in range(2):
            @pl.when((core == c) & (x0 == x))
            def _(c=c, x=x):
                if c == x:
                    pltpu.make_async_copy(leaf.at[:, c], slots[x].at[0], leaf_local).wait()
                    leaf_copy(1 - c, slots[x], (u_core, v), x).wait_send()
                    leaf_copy(0, slots[1 - x], (u_core, v), 1 - x).wait_recv()
                else:
                    for part in range(2):
                        leaf_copy(part, slots[x], (u_core, v), x).wait_send()
                    for slot in range(2):
                        leaf_copy(0, slots[slot], (u_core, v), slot).wait_recv()

    halo_start((2,), odd_v)
    halo_start((3,), even_v)
    straight_west, straight_east = jnp.logical_not(turn_west), jnp.logical_not(turn_east)

    def y_copy(t, part, to):
        span = slice(2 * part, 2 * part + 2)
        return pltpu.make_async_remote_copy(
            src_ref=mine.at[t + 1, span], dst_ref=other.at[t + 1, span],
            send_sem=y_send.at[t, part], recv_sem=y_recv.at[t, part],
            device_id=to, device_id_type=MESH,
        )

    def w_copy(t, to):
        return pltpu.make_async_remote_copy(
            src_ref=w_mine.at[t + 1], dst_ref=w_other.at[t + 1], send_sem=w_send.at[t], recv_sem=w_recv.at[t],
            device_id=to, device_id_type=MESH,
        )

    def cross_copy(t):
        return pltpu.make_async_remote_copy(
            src_ref=cross_send.at[t], dst_ref=cross_recv.at[t], send_sem=c_send.at[t], recv_sem=c_recv.at[t],
            device_id=(u_core, v), device_id_type=MESH,
        )

    def leaf_gram_copy(kind):
        return pltpu.make_async_remote_copy(
            src_ref=cross_send.at[LEVELS + kind], dst_ref=cross_recv.at[LEVELS + kind], send_sem=g_send.at[kind],
            recv_sem=g_recv.at[kind], device_id=(u_core, v), device_id_type=MESH,
        )

    def swap_copy():
        return pltpu.make_async_remote_copy(
            src_ref=path, dst_ref=swap, send_sem=s_send, recv_sem=s_recv,
            device_id=(u_core, v_next), device_id_type=MESH,
        )

    def row_copy(d):
        to = (v + d) % 16
        return pltpu.make_async_remote_copy(
            src_ref=term.at[to], dst_ref=from_row.at[d], send_sem=row_send.at[d], recv_sem=row_recv.at[d],
            device_id=(u, to), device_id_type=MESH,
        )

    out_copies = [
        pltpu.make_async_copy(out.at[:, 1:5], corrected.at[:, 1:5], out_sem.at[0]),
        pltpu.make_async_copy(out.at[:, 0], corrected.at[:, 0], out_sem.at[1]),
        pltpu.make_async_copy(out.at[:, 5], corrected.at[:, 5], out_sem.at[2]),
    ]

    def merge(t, carry):
        wide = widened(w_mine[t], w_other[t])
        for part in range(2):
            span = slice(2 * part, 2 * part + 2)
            both = dot_sum(mine[t, span].reshape(256, 128), other[t, span].reshape(256, 128), wide)
            mine[t + 1, span] = both.reshape(2, 128, 128)
            for step in range(LEVELS - 1):
                @pl.when(t == step)
                def _(step=step, part=part):
                    y_copy(step, part, partners[step + 1]).start()

        @pl.when(t == 1)
        def _():
            halo_start((4, 8), straight_west)
            halo_start((5, 9), straight_east)

        @pl.when(t == 2)
        def _():
            halo_start((6, 11), straight_west)
            halo_start((7, 10), straight_east)

        @pl.when(t == 3)
        def _():
            halo_start((6, 8, 11), turn_west)
            halo_start((7, 9, 10), turn_east)

        @pl.when(t == 0)
        def _():
            merged = mine[1].reshape(512, 128)
            part = dot_tn(merged, merged)
            cross_send[LEVELS] = part
            leaf_gram_copy(0).start()
            ours = dot_tn(merged, mine[0].reshape(512, 128))
            theirs = dot_tn(merged, other[0].reshape(512, 128))
            cross_send[LEVELS + 1] = jnp.where(core == 0, theirs, ours)
            leaf_gram_copy(1).start()
            leaf_gram_copy(0).wait()
            gram[...] = part + cross_recv[LEVELS]
            mixed[...] = jnp.where(core == 0, ours, theirs)

        @pl.when(t > 0)
        def _():
            mixed[...] = dot_nn(cross[...], w_other[t])
            half = dot_tn(w_mine[t], mixed[...])
            gram[...] = base[...] + half + half.T

        cholesky_inverse(gram, linv.at[t], panels)

        @pl.when(t < LEVELS - 1)
        def _():
            w_mine[t + 1] = dot_tn(linv[t], halves[t + 1])

        for step in range(LEVELS - 1):
            @pl.when(t == step)
            def _(step=step):
                w_copy(step, partners[step + 1]).start()

        @pl.when(t == 0)
        def _():
            leaf_gram_copy(1).wait()
            path[...] = mixed[...] + cross_recv[LEVELS + 1]

        @pl.when(t > 0)
        def _():
            path[...] = dot_tn(halves[t], path[...]) + dot_tn(mixed[...], dot_tn(linv[t - 1], path[...]))

        path[...] = dot_nn(linv[t], path[...])

        @pl.when(t < LEVELS - 1)
        def _():
            y_copy(t, 0, (u_core, v)).wait()
            part = dot_tn(mine[t + 1, 0:2].reshape(256, 128), other[t + 1, 0:2].reshape(256, 128))
            y_copy(t, 1, (u_core, v)).wait()
            part = part + dot_tn(mine[t + 1, 2:4].reshape(256, 128), other[t + 1, 2:4].reshape(256, 128))
            cross_send[t] = part
            cross_copy(t).start()

        @pl.when((t == 4) & (core != x0))
        def _():
            swap_copy().start()

        @pl.when(t == 0)
        def _():
            for copy in loads:
                copy.wait()
            halo_wait((0, 1))
            for a in (0, 7):
                for place, col in ((1, 0), (2, 1), (3, 4), (4, 5)):
                    ext[a, place] = inner[a, col]

        for step in range(4):
            @pl.when(t == step)
            def _(step=step):
                inner_pairs(INNER[step], INNER[step + 1])

        @pl.when(t == 4)
        def _():
            out_copies[0].start()
            halo_wait(range(2, 12))
            side_pairs(0, 3)

        @pl.when((t == 4) & (core != x0))
        def _():
            swap_copy().wait()
            path[...] = swap[...]

        @pl.when(t == 5)
        def _():
            side_pairs(3, 6)
            out_copies[1].start()
            out_copies[2].start()
            products = lax.dot_general(
                coef[...], path[...], (((0,), (1,)), ((), ())), precision=highest, preferred_element_type=f32
            )
            term[...] = products.reshape(16, 48, 128)
            for d in range(1, 16):
                row_copy(d).start()
            path[...] = diag_matrix()

        @pl.when(t < LEVELS - 1)
        def _():
            cross_copy(t).wait()
            cross[...] = cross_send[t] + cross_recv[t]
            w_copy(t, (u_core, v)).wait()

        return carry

    def diag_matrix():
        down_iota = lax.broadcasted_iota(jnp.int32, (128, 128), 0)
        return jnp.where(down_iota == lax.broadcasted_iota(jnp.int32, (128, 128), 1), 1.0, 0.0).astype(f32)

    lax.fori_loop(0, LEVELS, merge, 0)
    total = term[v]
    for d in range(1, 16):
        row_copy(d).wait()
        total = total + from_row[d]
    total = dot_nt(total, path[...])
    row_sum[...] = total
    copies = []
    for d in range(1, 8):
        copy = pltpu.make_async_remote_copy(
            src_ref=row_sum, dst_ref=from_col.at[d], send_sem=col_send.at[d], recv_sem=col_recv.at[d],
            device_id=((u + d) % 8, v), device_id_type=MESH,
        )
        copy.start()
        copies.append(copy)
    root = dot_nt(mine[LEVELS, y], linv[LEVELS - 1])
    for copy in out_copies:
        copy.wait()
    for d in range(1, 8):
        copies[d - 1].wait()
        total = total + from_col[d]
    far_out[...] = dot_nt(root, total)


def solve(links, density, near_blocks, far_right, far_left, sketch, keys):
    anywhere = pl.BlockSpec(memory_space=pl.ANY)
    vmem = pl.BlockSpec(memory_space=pltpu.VMEM)
    dma = pltpu.SemaphoreType.DMA
    bf16 = jnp.bfloat16
    return pl.pallas_call(
        solver_kernel,
        out_shape=(jax.ShapeDtypeStruct((6, 6, 128, 768), bf16), jax.ShapeDtypeStruct((128, 48), f32)),
        in_specs=[pl.BlockSpec(memory_space=pltpu.SMEM)] + [anywhere] * 4 + [vmem, vmem],
        out_specs=(anywhere, vmem),
        scratch_shapes=[
            pltpu.VMEM((9, 6, 128, 768), bf16),
            pltpu.VMEM((9, 6, 128, 768), bf16),
            pltpu.VMEM((6, 6, 6, 128, 128), bf16),
            pltpu.VMEM((6, 6, 128, 128), bf16),
            pltpu.VMEM((6, 6, 128, 768), bf16),
            pltpu.VMEM((128, 768), f32),
            pltpu.VMEM((LEVELS + 1, 4, 128, 128), f32),
            pltpu.VMEM((LEVELS + 1, 4, 128, 128), f32),
            pltpu.VMEM((LEVELS + 1, 128, 128), f32),
            pltpu.VMEM((LEVELS + 1, 128, 128), f32),
            pltpu.VMEM((LEVELS, 128, 128), f32),
            pltpu.VMEM((128, 128), f32),
            pltpu.VMEM((LEVELS + 2, 128, 128), f32),
            pltpu.VMEM((LEVELS + 2, 128, 128), f32),
            pltpu.VMEM((128, 128), f32),
            pltpu.VMEM((128, 128), f32),
            pltpu.VMEM((128, 128), f32),
            pltpu.VMEM((16, 10, 8, 128), f32),
            pltpu.VMEM((LEVELS, 128, 128), f32),
            pltpu.VMEM((128, 128), f32),
            pltpu.VMEM((128, 128), f32),
            pltpu.VMEM((16, 48, 128), f32),
            pltpu.VMEM((16, 48, 128), f32),
            pltpu.VMEM((48, 128), f32),
            pltpu.VMEM((8, 48, 128), f32),
            dma((5,)), dma((3,)), dma((12,)), dma((12,)),
            dma, dma((2,)), dma((2,)),
            dma((LEVELS, 2)), dma((LEVELS, 2)), dma((LEVELS,)), dma((LEVELS,)),
            dma((LEVELS,)), dma((LEVELS,)), dma((2,)), dma((2,)), dma, dma,
            dma((16,)), dma((16,)), dma((8,)), dma((8,)),
        ],
        compiler_params=pltpu.CompilerParams(collective_id=0, has_side_effects=True, vmem_limit_bytes=60 * 2**20),
        cost_estimate=pl.CostEstimate(flops=10**10, bytes_accessed=2**25, transcendentals=0),
        name="solver",
    )(links, density, near_blocks, far_right, far_left.reshape(4, 2, 128, 128), sketch, keys)


def copy_kernel(source, target, held, in_sem, out_sem):
    reads = [pltpu.make_async_copy(source.at[i], held.at[i], in_sem.at[i]) for i in range(6)]
    writes = [pltpu.make_async_copy(held.at[i], target.at[i], out_sem.at[i]) for i in range(6)]
    for copy in reads:
        copy.start()
    for read, write in zip(reads, writes):
        read.wait()
        write.start()
    for copy in writes:
        copy.wait()


def copied(value):
    anywhere = pl.BlockSpec(memory_space=pl.ANY)
    return pl.pallas_call(
        copy_kernel,
        out_shape=jax.ShapeDtypeStruct(value.shape, value.dtype),
        in_specs=[anywhere],
        out_specs=anywhere,
        scratch_shapes=[
            pltpu.VMEM(value.shape, value.dtype), pltpu.SemaphoreType.DMA((6,)), pltpu.SemaphoreType.DMA((6,)),
        ],
        compiler_params=pltpu.CompilerParams(vmem_limit_bytes=60 * 2**20),
        name="copy_out",
    )(value)


def per_device(density, near_blocks, neighbours, far_right, far_left, sketch, patch_order):
    corrected, far_field = solve(
        neighbours, density, near_blocks, far_right, far_left, sketch, patch_order.reshape(1, 128)
    )
    return (copied(corrected), far_field)


def solution(mesh):
    in_specs = (
        P("pu", "pv", None, None),
        P("pu", "pv", None, None, None),
        P("pu", "pv", None),
        P("pu", "pv", None, None),
        P("pu", "pv", None, None),
        P(),
        P(),
    )
    out_specs = (P("pu", "pv", None, None), P("pu", "pv"))
    return jax.shard_map(
        per_device, mesh=mesh, in_specs=in_specs, out_specs=out_specs, check_vma=False
    )
```
